512 devices in a mesh: row: 16 (over y, z_hi), col: 32 (over z_lo, x, core).
Axes of the slice: x: 4, y: 4, z: 16 (z_hi: 4, z_lo: 4; z = z_hi * 4 + z_lo), core: 2. Of those that a mesh axis runs over, the one named last changes fastest.
Arguments:
- vectors: bfloat16 [49152, 128], P('row'), may hold values from -6 to 6
- tiles: bfloat16 [4096, 256, 256], P(('row', 'col')), may hold values from -0.0546875 to 0.0546875
- tile_rows: int32 [4096], P(('row', 'col')), may hold values from 0 to 191, as said below
- tile_cols: int32 [4096], P(('row', 'col')), may hold values from 0 to 191, as said below
Outputs:
- applied: bfloat16 [49152, 128], P(('row', 'col'))
- applied_twice: bfloat16 [49152, 128], P(('row', 'col'))
- gram_norm: float32 [128, 128], replicated
- gram_rayleigh: float32 [128, 128], replicated
The draws below stay inside these ranges and needn't reach their ends.
Inputs may be any that keep to these rules, and one draw needn't show every extreme that they name: `tile_rows`: let G = 16. Tiles k in [d * 8, (d + 1) * 8) lie on the device d = r * 32 + c; with p = c % G, that device's tiles have block rows in [max(r, p) * 12, (max(r, p) + 1) * 12) and block columns in [min(r, p) * 12, (min(r, p) + 1) * 12); where r equals p the block row is at least the block column. No position occurs twice. `tile_cols`: the block columns of the tiles described with tile_rows.
All inputs are finite; a program needn't handle non-finite values.
Results may differ from the reference program's by a relative error of at most 0.0039.
Values may be sent and summed in bfloat16 or wider, within the bound.
A program may use at most 64 MiB of HBM per device.

```python
import jax
import jax.numpy as jnp
from jax import lax

TS = 256
V = 128
B = 12
TILES_DEV = 8
NROWS = 49152
TILES = 4096
N_ROW = 16
N_COL = 32


def tile_layout(key):
    devices_all = jnp.arange(N_ROW * N_COL, dtype=jnp.int32)
    row_index = devices_all // N_COL
    col_index = devices_all % N_COL
    partner = col_index % N_ROW
    half_index = col_index // N_ROW
    group_hi = jnp.maximum(row_index, partner)
    group_lo = jnp.minimum(row_index, partner)
    slot = jnp.where(row_index >= partner, half_index, 2 + half_index)
    pair_id = group_hi * N_ROW + group_lo

    def one_device(pair_key, slot_one, high, low):
        sub_key = jax.random.fold_in(key, pair_key)
        scores = jax.random.randint(sub_key, (B * B,), 0, 65536)
        position = jnp.arange(B * B, dtype=jnp.int32)
        local_row = position // B
        local_col = position % B
        upper = (high == low) & (local_col > local_row)
        ranked = scores * (B * B) + position + jnp.where(upper, 65536 * (B * B), 0)
        order = jnp.argsort(ranked, stable=True).astype(jnp.int32)
        picked = lax.dynamic_slice(order, (slot_one * TILES_DEV,), (TILES_DEV,))
        return (high * B + picked // B, low * B + picked % B)
    rows_all, cols_all = jax.vmap(one_device)(pair_id, slot, group_hi, group_lo)
    return (rows_all.reshape(-1).astype(jnp.int32), cols_all.reshape(-1).astype(jnp.int32))


def draw_tile_rows(key, part):
    rows_all, cols_all = tile_layout(key)
    return rows_all


def draw_tile_cols(key, part):
    rows_all, cols_all = tile_layout(key)
    return cols_all


def block_scale(key, shape, shards, smallest, largest):
    level = 1.0
    for dim, parts in shards:
        draws = jax.random.uniform(jax.random.fold_in(jax.random.fold_in(key, 6), dim), (parts,), jnp.float32, smallest / len(shards), largest / len(shards))
        level = level * jnp.repeat(jnp.exp(draws), shape[dim] // parts).reshape((-1,) + (1,) * (len(shape) - 1 - dim))
    return level


def normal_values(own_key, dims, deviation, limit, shards=(), held_as=jnp.bfloat16):
    level = block_scale(own_key, dims, shards, -0.22, 0.18) if shards else 1.0
    array = jax.random.normal(own_key, dims, jnp.float32) * deviation * level
    return jnp.minimum(jnp.maximum(array, -limit), limit).astype(held_as)


def setup_inputs(seed: int = 0) -> dict:
    key_list = jax.random.split(jax.random.key(seed), 5)
    return {
        "vectors": normal_values(key_list[0], (NROWS, V), 1.0, 6.0, ((0, 16),)),
        "tiles": normal_values(key_list[1], (TILES, TS, TS), (2 * TILES_DEV * N_COL * TS // B) ** -0.5, 0.0546875, ((0, 512),)),
        "tile_rows": draw_tile_rows(jax.random.fold_in(key_list[4], 71), 0),
        "tile_cols": draw_tile_cols(jax.random.fold_in(key_list[4], 71), 0),
    }


def apply_h(vec, tiles, tile_rows, tile_cols):
    nblocks = vec.shape[0] // TS
    blocks = vec.reshape(nblocks, TS, V).astype(jnp.float32)
    per_step = TILES_DEV * N_COL
    steps = tile_rows.shape[0] // per_step
    tile_sets = tiles.reshape(steps, per_step, TS, TS)
    row_sets = tile_rows.reshape(steps, per_step)
    col_sets = tile_cols.reshape(steps, per_step)

    def step(acc, item):
        tile_set, row_set, col_set = item
        tile_f = tile_set.astype(jnp.float32)
        forward_part = jnp.einsum("kab,kbv->kav", tile_f, blocks[col_set], precision=lax.Precision.HIGHEST)
        backward_part = jnp.einsum("kba,kbv->kav", tile_f, blocks[row_set], precision=lax.Precision.HIGHEST)
        acc = acc.at[row_set].add(forward_part)
        acc = acc.at[col_set].add(backward_part)
        return acc, None

    start = jnp.zeros((nblocks, TS, V), jnp.float32)
    total, _ = lax.scan(step, start, (tile_sets, row_sets, col_sets))
    return total.reshape(nblocks * TS, V).astype(jnp.bfloat16)


def reference(vectors, tiles, tile_rows, tile_cols):
    applied = apply_h(vectors, tiles, tile_rows, tile_cols)
    applied_twice = apply_h(applied, tiles, tile_rows, tile_cols)
    gram_norm = jnp.dot(applied.T, applied, preferred_element_type=jnp.float32) / NROWS
    gram_rayleigh = jnp.dot(applied.T, applied_twice, preferred_element_type=jnp.float32) / NROWS
    return applied, applied_twice, gram_norm, gram_rayleigh
```

```python
import jax
import jax.numpy as jnp
from jax import lax
from jax.experimental import pallas as pl
from jax.experimental.pallas import tpu as pltpu
from jax.sharding import PartitionSpec as P

MESH = pl.DeviceIdType.MESH
BF = jnp.bfloat16
F32 = jnp.float32
TS = 256
V = 128
NB = 12
G = 16
NCOL = 32
K = 8
GROUP = NB * TS
CH = GROUP // NCOL
QU = GROUP // 4
NROWS = GROUP * G

ZIN, YIN, YRS, ZOUT, OOUT, OIN, G1, G2, G3 = range(9)


def loop(n, body):
    def step(i, carry):
        body(i)
        return carry

    lax.fori_loop(0, n, step, 0)


def kernel(
    vec, tiles, trows, tcols, out1, out2, gn, gr,
    tt, up0, up1, uo, prod, pb, ob, yr, zs, zr, orr, ach, gs, gr1, gp, gr2, gf, ga,
    ssem, rsem,
):
    up = (up0, up1)
    r = lax.axis_index("row")
    c = lax.axis_index("col")
    y, zh = r // 4, r % 4
    zl = c // 8
    p = c % G
    is_high = p <= r
    self_z = jnp.logical_and(p == r, y == zl)

    def wait_bytes(ref, sem):
        pltpu.make_async_copy(ref, ref, sem).wait()

    def z_group(i):
        return 4 * zl + i // 2, r + G * (i % 2)

    def z_owner(i):
        return p, 8 * y + i

    barrier = pltpu.get_barrier_semaphore()

    def greet(row, col):
        pl.semaphore_signal(barrier, inc=1, device_id=(row, col), device_id_type=MESH)

    def greet_other(row, col):
        @pl.when(jnp.logical_or(row != r, col != c))
        def _():
            greet(row, col)

    loop(NCOL - 1, lambda i: greet(r, (c + i + 1) % NCOL))
    loop(G - 1, lambda i: greet((r + i + 1) % G, c))
    loop(8, lambda i: greet_other(*z_group(i)))
    loop(8, lambda i: greet_other(*z_owner(i)))

    straight = jnp.where(is_high, 0, 1)

    def turn(k):
        t = tiles[k]
        tt[straight, k] = t
        tt[1 - straight, k] = t.T

    loop(K, turn)

    def within(block):
        return jnp.minimum(jnp.maximum(block, 0), NB - 1)

    def own_id(k):
        return within(jnp.where(is_high, trows[k], tcols[k]) - r * NB)

    def par_id(k):
        return within(jnp.where(is_high, tcols[k], trows[k]) - p * NB)

    pl.semaphore_wait(barrier, NCOL - 1 + G - 1 + 16 - 2 * jnp.where(self_z, 1, 0))

    def send(src, dst, a, stage, row, col):
        pltpu.make_async_remote_copy(
            src_ref=src,
            dst_ref=dst,
            send_sem=ssem.at[a, stage],
            recv_sem=rsem.at[a, stage],
            device_id=(row, col),
            device_id_type=MESH,
        ).start()

    def send_or_copy(src, dst, a, stage, row, col):
        same = jnp.logical_and(row == r, col == c)

        @pl.when(same)
        def _():
            pltpu.make_async_copy(src, dst, rsem.at[a, stage]).start()

        @pl.when(jnp.logical_not(same))
        def _():
            send(src, dst, a, stage, row, col)

    def rows(ref, start, count):
        return ref.at[pl.ds(pl.multiple_of(start, 32), count)]

    def z_in(a, src):
        def body(i):
            send_or_copy(src, rows(up[a], c * CH, CH), a, ZIN, *z_group(i))

        loop(8, body)

    def y_in(a):
        wait_bytes(up[a].at[pl.ds(0, QU)], rsem.at[a, ZIN])
        part = rows(up[a], y * QU, QU)

        def body(i):
            send(part, part, a, YIN, 4 * ((y + i + 1) % 4) + zh, c)

        loop(3, body)

    def own_in(a):
        def body(i):
            send(ach, rows(uo, c * CH, CH), a, OIN, r, (c + i + 1) % NCOL)

        loop(NCOL - 1, body)

    def one_if_same(left, right):
        gap = left - right
        return (1 - jnp.minimum(gap * gap, 1)).astype(F32)

    def products(side, ids_from, source, ids_to, target):
        def one(k):
            block = source[pl.ds(ids_from(k) * TS, TS), :]
            prod[k] = jnp.dot(tt[side, k], block, preferred_element_type=F32)

        loop(K, one)

        def gather(b):
            weights = [one_if_same(ids_to(k), b) for k in range(K)]
            for q in range(4):
                piece = pl.ds(64 * q, 64)
                acc = prod[0, piece, :] * weights[0]
                for k in range(1, K):
                    acc = acc + prod[k, piece, :] * weights[k]
                target[pl.ds(pl.multiple_of(b * TS + 64 * q, 64), 64), :] = acc.astype(BF)

        loop(NB, gather)

    def y_out(a):
        def body(i):
            to = (y + i + 1) % 4
            send(rows(pb.at[a], to * QU, QU), yr.at[a, i], a, YRS, 4 * to + zh, c)

        loop(3, body)

    def z_out(a):
        wait_bytes(yr.at[a], rsem.at[a, YRS])

        def add(j):
            at = pl.multiple_of(j * CH, CH)
            acc = pb[a, pl.ds(pl.multiple_of(y * QU + j * CH, CH), CH), :].astype(F32)
            for i in range(3):
                acc = acc + yr[a, i, pl.ds(at, CH), :].astype(F32)
            zs[a, pl.ds(at, CH), :] = acc.astype(BF)

        loop(8, add)
        slot = zh * 2 + c // G

        def body(i):
            send_or_copy(rows(zs.at[a], i * CH, CH), zr.at[a, slot], a, ZOUT, *z_owner(i))

        loop(8, body)

    def own_out(a):
        def body(i):
            to = (c + i + 1) % NCOL
            send(rows(ob.at[a], to * CH, CH), orr.at[a, i], a, OOUT, r, to)

        loop(NCOL - 1, body)

    def total(a):
        wait_bytes(orr.at[a], rsem.at[a, OOUT])
        wait_bytes(zr.at[a], rsem.at[a, ZOUT])
        acc = ob[a, pl.ds(pl.multiple_of(c * CH, CH), CH), :].astype(F32)
        acc = lax.fori_loop(0, NCOL - 1, lambda i, s: s + orr[a, i].astype(F32), acc)
        acc = lax.fori_loop(0, 8, lambda i, s: s + zr[a, i].astype(F32), acc)
        return acc.astype(BF)

    def inner(left, right):
        return lax.dot_general(left, right, (((0,), (0,)), ((), ())), preferred_element_type=F32)

    z_in(0, rows(vec, c * CH, CH))
    products(1, own_id, vec, par_id, pb.at[0])
    y_out(0)
    y_in(0)
    z_out(0)
    wait_bytes(up[0].at[pl.ds(0, 3 * QU)], rsem.at[0, YIN])
    products(0, par_id, up[0], own_id, ob.at[0])
    own_out(0)
    first = total(0)
    ach[...] = first
    out1[...] = first

    z_in(1, ach)
    own_in(1)
    uo[pl.ds(pl.multiple_of(c * CH, CH), CH), :] = first
    gs[pl.ds(0, V), :] = inner(first, first)
    y_in(1)
    wait_bytes(uo.at[pl.ds(0, GROUP - CH)], rsem.at[1, OIN])
    products(1, own_id, uo, par_id, pb.at[1])
    y_out(1)
    wait_bytes(up[1].at[pl.ds(0, 3 * QU)], rsem.at[1, YIN])
    products(0, par_id, up[1], own_id, ob.at[1])
    own_out(1)

    gs[pl.ds(V, V), :] = inner(uo[...], ob[1]) + inner(up[1][...], pb[1])

    def gram_out(i):
        to = (c + i + 1) % NCOL
        send(gs.at[pl.ds(pl.multiple_of(to * 8, 8), 8)], gr1.at[i], 1, G1, r, to)

    loop(NCOL - 1, gram_out)
    z_out(1)

    wait_bytes(gr1, rsem.at[1, G1])
    acc = gs[pl.ds(pl.multiple_of(c * 8, 8), 8), :]
    gp[...] = lax.fori_loop(0, NCOL - 1, lambda i, s: s + gr1[i], acc)
    loop(G - 1, lambda i: send(gp, gr2.at[i], 1, G2, (r + i + 1) % G, c))
    second = total(1)
    out2[...] = second

    wait_bytes(gr2, rsem.at[1, G2])
    acc = lax.fori_loop(0, G - 1, lambda i, s: s + gr2[i], gp[...])
    gf[...] = acc
    mine = pl.ds(pl.multiple_of(c * 8, 8), 8)
    loop(NCOL - 1, lambda i: send(gf, ga.at[mine], 1, G3, r, (c + i + 1) % NCOL))
    ga[mine, :] = acc
    wait_bytes(ga.at[pl.ds(0, 2 * V - 8)], rsem.at[1, G3])
    gn[...] = ga[pl.ds(0, V), :] / NROWS
    gr[...] = ga[pl.ds(V, V), :] / NROWS

    for a in range(2):
        @pl.when(self_z)
        def _():
            wait_bytes(up[a].at[pl.ds(0, 7 * CH)], ssem.at[a, ZIN])
            wait_bytes(up[a].at[pl.ds(0, 7 * CH)], ssem.at[a, ZOUT])

        @pl.when(jnp.logical_not(self_z))
        def _():
            wait_bytes(up[a].at[pl.ds(0, 8 * CH)], ssem.at[a, ZIN])
            wait_bytes(up[a].at[pl.ds(0, 8 * CH)], ssem.at[a, ZOUT])

        wait_bytes(up[a].at[pl.ds(0, 3 * QU)], ssem.at[a, YIN])
        wait_bytes(yr.at[a], ssem.at[a, YRS])
        wait_bytes(orr.at[a], ssem.at[a, OOUT])
    wait_bytes(orr.at[1], ssem.at[1, OIN])
    wait_bytes(gr1, ssem.at[1, G1])
    wait_bytes(gr2, ssem.at[1, G2])
    wait_bytes(gr1, ssem.at[1, G3])


def body(vectors, tiles, tile_rows, tile_cols):
    vmem = pl.BlockSpec(memory_space=pltpu.VMEM)
    smem = pl.BlockSpec(memory_space=pltpu.SMEM)
    return pl.pallas_call(
        kernel,
        out_shape=(
            jax.ShapeDtypeStruct((CH, V), BF),
            jax.ShapeDtypeStruct((CH, V), BF),
            jax.ShapeDtypeStruct((V, V), F32),
            jax.ShapeDtypeStruct((V, V), F32),
        ),
        in_specs=[vmem, vmem, smem, smem],
        out_specs=(vmem,) * 4,
        scratch_shapes=[
            pltpu.VMEM((2, K, TS, TS), BF),
            pltpu.VMEM((GROUP, V), BF),
            pltpu.VMEM((GROUP, V), BF),
            pltpu.VMEM((GROUP, V), BF),
            pltpu.VMEM((K, TS, V), F32),
            pltpu.VMEM((2, GROUP, V), BF),
            pltpu.VMEM((2, GROUP, V), BF),
            pltpu.VMEM((2, 3, QU, V), BF),
            pltpu.VMEM((2, QU, V), BF),
            pltpu.VMEM((2, 8, CH, V), BF),
            pltpu.VMEM((2, NCOL - 1, CH, V), BF),
            pltpu.VMEM((CH, V), BF),
            pltpu.VMEM((2 * V, V), F32),
            pltpu.VMEM((NCOL - 1, 8, V), F32),
            pltpu.VMEM((8, V), F32),
            pltpu.VMEM((G - 1, 8, V), F32),
            pltpu.VMEM((8, V), F32),
            pltpu.VMEM((2 * V, V), F32),
            pltpu.SemaphoreType.DMA((2, 9)),
            pltpu.SemaphoreType.DMA((2, 9)),
        ],
        compiler_params=pltpu.CompilerParams(
            collective_id=0, has_side_effects=True, vmem_limit_bytes=40 * 2**20
        ),
    )(vectors, tiles, tile_rows, tile_cols)


def solution(mesh):
    placed = (P("row", None), P(("row", "col"), None, None), P(("row", "col")), P(("row", "col")))
    return jax.shard_map(
        body,
        mesh=mesh,
        in_specs=placed,
        out_specs=(P(("row", "col"), None), P(("row", "col"), None), P(), P()),
        check_vma=False,
    )
```

```python
import jax
import jax.numpy as jnp
from jax import lax
from jax.experimental import pallas as pl
from jax.experimental.pallas import tpu as pltpu
from jax.sharding import PartitionSpec as P

MESH = pl.DeviceIdType.MESH
BF = jnp.bfloat16
F32 = jnp.float32
TS = 256
V = 128
NB = 12
G = 16
NCOL = 32
K = 8
GROUP = NB * TS
CH = GROUP // NCOL
QU = GROUP // 4
NROWS = GROUP * G

ZIN, YIN, YRS, ZOUT, OZ, OX, XRS, OOUT, G1, G2, G3 = range(11)
NSTAGE = 11


def loop(n, body):
    def step(i, carry):
        body(i)
        return carry

    lax.fori_loop(0, n, step, 0)


def kernel(
    vec_in, tiles_in, trows, tcols, out1, out2, gn, gr,
    vec, tiles, tt, up0, up1, uo, prod, pb, ob, yr, xr, zs, zr, osum, orr, ach,
    gs, gr1, gp, gr2, gf, ga, ssem, rsem, lsem,
):
    up = (up0, up1)
    r = lax.axis_index("row")
    c = lax.axis_index("col")
    y, zh = r // 4, r % 4
    zl, xk = c // 8, c % 8
    x, k = xk // 2, c % 2
    x1 = x + 1 - 2 * (x % 2)
    par = zl % 2
    p = c % G
    p1 = 8 * par + 2 * x1 + k
    is_high = p <= r
    to_xk = 2 * ((x + 2 * (y // 2)) % 4) + y % 2
    self_z = jnp.logical_and(p == r, y == zl)
    self_out = jnp.logical_and(jnp.logical_or(p == r, p1 == r), to_xk == xk)

    load_vec = pltpu.make_async_copy(vec_in, vec, lsem.at[0])
    load_tiles = pltpu.make_async_copy(tiles_in, tiles, lsem.at[1])
    load_vec.start()
    load_tiles.start()

    def wait_bytes(ref, sem):
        pltpu.make_async_copy(ref, ref, sem).wait()

    def z_group(i):
        return 4 * zl + (zh + 2 + i // 2) % 4, r + G * (i % 2)

    def z_owner(i):
        return p, 8 * y + i

    def out_owner(q, e):
        return (p if e == 0 else p1), 8 * q + to_xk

    rx, rk, rpar = (r // 2) % 4, r % 2, r // 8
    flip = (x % 2 + rx % 2) % 2
    from_y = 2 * ((x // 2 + rx // 2) % 2) + k
    from_x = rx + flip * (1 - 2 * (rx % 2))

    def out_source(i):
        return 4 * from_y + i // 2, 8 * (rpar + 2 * (i % 2)) + 2 * from_x + rk

    def pair_mate(j):
        return 4 * j + zh, 8 * zl + 2 * x1 + k

    barrier = pltpu.get_barrier_semaphore()

    def greet(row, col):
        pl.semaphore_signal(barrier, inc=1, device_id=(row, col), device_id_type=MESH)

    def greet_other(row, col):
        @pl.when(jnp.logical_or(row != r, col != c))
        def _():
            greet(row, col)

    loop(8, lambda i: greet_other(*z_group(i)))
    loop(8, lambda i: greet_other(*z_owner(i)))
    loop(4, lambda q: greet_other(*out_owner(q, 0)))
    loop(4, lambda q: greet_other(*out_owner(q, 1)))
    loop(8, lambda i: greet_other(*out_source(i)))
    loop(G - 1, lambda i: greet((r + i + 1) % G, c))
    loop(4, lambda j: greet(*pair_mate(j)))
    loop(NCOL - 1, lambda i: greet(r, (c + i + 1) % NCOL))

    straight = jnp.where(is_high, 0, 1)
    load_vec.wait()
    load_tiles.wait()

    def turn(k):
        t = tiles[k]
        tt[straight, k] = t
        tt[1 - straight, k] = t.T

    loop(K, turn)

    def within(block):
        return jnp.minimum(jnp.maximum(block, 0), NB - 1)

    def own_id(k):
        return within(jnp.where(is_high, trows[k], tcols[k]) - r * NB)

    def par_id(k):
        return within(jnp.where(is_high, tcols[k], trows[k]) - p * NB)

    def send(src, dst, a, stage, sub, row, col):
        pltpu.make_async_remote_copy(
            src_ref=src,
            dst_ref=dst,
            send_sem=ssem.at[a, stage],
            recv_sem=rsem.at[a, stage, sub],
            device_id=(row, col),
            device_id_type=MESH,
        ).start()

    def send_or_copy(src, dst, a, stage, sub, row, col):
        same = jnp.logical_and(row == r, col == c)

        @pl.when(same)
        def _():
            pltpu.make_async_copy(src, dst, rsem.at[a, stage, sub]).start()

        @pl.when(jnp.logical_not(same))
        def _():
            send(src, dst, a, stage, sub, row, col)

    def chunk(ref, i):
        return ref.at[pl.ds(pl.multiple_of(i * CH, CH), CH)]

    def read(ref, a, i):
        return ref[a, pl.ds(pl.multiple_of(i * CH, CH), CH), :].astype(F32)

    def z_in(a, src):
        loop(8, lambda i: send_or_copy(src, chunk(up[a], c), a, ZIN, xk, *z_group(i)))

    def y_in(a):
        def forward(i):
            part = chunk(up[a], 8 * y + i)
            wait_bytes(part, rsem.at[a, ZIN, i])
            loop(3, lambda j: send(part, part, a, YIN, 0, 4 * ((y + j + 1) % 4) + zh, c))

        loop(8, forward)

    def to_mates(src, where):
        loop(7, lambda i: send(src, chunk(uo, where), 1, OX, 0, r, 8 * zl + (xk + i + 1) % 8))

    def own_in():
        loop(3, lambda i: send(ach, chunk(uo, c), 1, OZ, i, r, 8 * ((zl + i + 1) % 4) + xk))
        to_mates(ach, c)

        def forward(i):
            cc = 8 * ((zl + 3 - i) % 4) + xk
            part = chunk(uo, cc)
            wait_bytes(part, rsem.at[1, OZ, i])
            to_mates(part, cc)

        loop(3, forward)

    def one_if_same(left, right):
        gap = left - right
        return (1 - jnp.minimum(gap * gap, 1)).astype(F32)

    def multiply(side, ids_from, source):
        def one(k):
            block = source[pl.ds(ids_from(k) * TS, TS), :]
            prod[k] = jnp.dot(tt[side, k], block, preferred_element_type=F32)

        loop(K, one)

    def gather(ids_to, target, a, q):
        def block(i):
            b = 3 * q + i
            weights = [one_if_same(ids_to(k), b) for k in range(K)]
            for s in range(4):
                piece = pl.ds(64 * s, 64)
                acc = prod[0, piece, :] * weights[0]
                for k in range(1, K):
                    acc = acc + prod[k, piece, :] * weights[k]
                target[a, pl.ds(pl.multiple_of(b * TS + 64 * s, 64), 64), :] = acc.astype(BF)

        loop(3, block)

    def y_out(a, q):
        def mate(i):
            j = (y + i + 1) % 4
            part = chunk(pb.at[a], 8 * q + 2 * ((x + 2 * (j // 2)) % 4) + j % 2)
            send(part, yr.at[a, q, i], a, YRS, q, 4 * j + zh, c)

        def pair(i):
            j = (y + i) % 4
            part = chunk(pb.at[a], 8 * q + 2 * ((x1 + 2 * (j // 2)) % 4) + j % 2)
            send(part, yr.at[a, q, 3 + i], a, YRS, q, *pair_mate(j))

        loop(4, pair)
        loop(3, mate)

    def z_out(a):
        slot = zh * 2 + c // G

        def step(q):
            wait_bytes(yr.at[a, q], rsem.at[a, YRS, q])
            acc = read(pb, a, 8 * q + to_xk)
            for i in range(3):
                acc = acc + yr[a, q, i].astype(F32)
            zs[a, q, 0] = acc.astype(BF)
            acc = yr[a, q, 3].astype(F32)
            for i in range(4, 7):
                acc = acc + yr[a, q, i].astype(F32)
            zs[a, q, 1] = acc.astype(BF)
            send_or_copy(zs.at[a, q, 0], zr.at[a, slot], a, ZOUT, 0, *out_owner(q, 0))
            send_or_copy(zs.at[a, q, 1], zr.at[a, slot], a, ZOUT, 0, *out_owner(q, 1))

        loop(4, step)

    def x_out(a, q):
        def mate(i):
            to = (xk + i + 1) % 8
            send(chunk(ob.at[a], 8 * q + to), xr.at[a, q, i], a, XRS, q, r, 8 * zl + to)

        loop(7, mate)

    def own_sum(a, q):
        wait_bytes(xr.at[a, q], rsem.at[a, XRS, q])
        acc = read(ob, a, 8 * q + xk)
        for i in range(7):
            acc = acc + xr[a, q, i].astype(F32)
        osum[a, q] = acc

    def own_out(a):
        def step(i):
            q = (zl + i + 1) % 4
            own_sum(a, q)
            send(osum.at[a, q], orr.at[a, i], a, OOUT, 0, r, 8 * q + xk)

        loop(3, step)
        own_sum(a, zl)

    def total(a):
        wait_bytes(orr.at[a], rsem.at[a, OOUT, 0])
        wait_bytes(zr.at[a], rsem.at[a, ZOUT, 0])
        acc = osum[a, zl]
        for i in range(3):
            acc = acc + orr[a, i]
        for i in range(8):
            acc = acc + zr[a, i].astype(F32)
        return acc.astype(BF)

    def inner(left, right):
        return lax.dot_general(left, right, (((0,), (0,)), ((), ())), preferred_element_type=F32)

    multiply(1, own_id, vec)
    loop(4, lambda q: gather(par_id, pb, 0, q))
    waits = NCOL - 1 + G - 1 + 4 + 32
    pl.semaphore_wait(
        barrier, waits - 2 * jnp.where(self_z, 1, 0) - 2 * jnp.where(self_out, 1, 0)
    )
    z_in(0, chunk(vec, c))
    loop(4, lambda q: y_out(0, q))
    z_out(0)
    y_in(0)
    wait_bytes(up[0].at[pl.ds(0, 3 * QU)], rsem.at[0, YIN, 0])
    multiply(0, par_id, up[0])

    def finish_own(a):
        def step(i):
            q = (zl + i + 1) % 4
            gather(own_id, ob, a, q)
            x_out(a, q)

        loop(4, step)

    finish_own(0)
    own_out(0)
    first = total(0)
    ach[...] = first
    out1[...] = first

    z_in(1, ach)
    own_in()
    uo[pl.ds(pl.multiple_of(c * CH, CH), CH), :] = first
    gs[pl.ds(0, V), :] = inner(first, first)
    wait_bytes(uo.at[pl.ds(0, 28 * CH)], rsem.at[1, OX, 0])
    multiply(1, own_id, uo)

    def partner_step(q):
        gather(par_id, pb, 1, q)
        y_out(1, q)

    loop(4, partner_step)
    y_in(1)
    z_out(1)
    wait_bytes(up[1].at[pl.ds(0, 3 * QU)], rsem.at[1, YIN, 0])
    multiply(0, par_id, up[1])
    finish_own(1)

    gs[pl.ds(V, V), :] = inner(uo[...], ob[1]) + inner(up[1][...], pb[1])

    def gram_out(i):
        to = (c + i + 1) % NCOL
        send(gs.at[pl.ds(pl.multiple_of(to * 8, 8), 8)], gr1.at[i], 1, G1, 0, r, to)

    loop(NCOL - 1, gram_out)
    own_out(1)

    wait_bytes(gr1, rsem.at[1, G1, 0])
    acc = gs[pl.ds(pl.multiple_of(c * 8, 8), 8), :]
    gp[...] = lax.fori_loop(0, NCOL - 1, lambda i, s: s + gr1[i], acc)
    loop(G - 1, lambda i: send(gp, gr2.at[i], 1, G2, 0, (r + i + 1) % G, c))
    second = total(1)
    out2[...] = second

    wait_bytes(gr2, rsem.at[1, G2, 0])
    acc = lax.fori_loop(0, G - 1, lambda i, s: s + gr2[i], gp[...])
    gf[...] = acc
    mine = pl.ds(pl.multiple_of(c * 8, 8), 8)
    loop(NCOL - 1, lambda i: send(gf, ga.at[mine], 1, G3, 0, r, (c + i + 1) % NCOL))
    ga[mine, :] = acc
    wait_bytes(ga.at[pl.ds(0, 2 * V - 8)], rsem.at[1, G3, 0])
    gn[...] = ga[pl.ds(0, V), :] / NROWS
    gr[...] = ga[pl.ds(V, V), :] / NROWS

    def sent(a, stage, less, chunks):
        @pl.when(less)
        def _():
            wait_bytes(up[a].at[pl.ds(0, (chunks - 1) * CH)], ssem.at[a, stage])

        @pl.when(jnp.logical_not(less))
        def _():
            wait_bytes(up[a].at[pl.ds(0, chunks * CH)], ssem.at[a, stage])

    for a in range(2):
        sent(a, ZIN, self_z, 8)
        sent(a, ZOUT, self_out, 8)
        wait_bytes(up[a].at[pl.ds(0, 24 * CH)], ssem.at[a, YIN])
        wait_bytes(yr.at[a], ssem.at[a, YRS])
        wait_bytes(xr.at[a], ssem.at[a, XRS])
        wait_bytes(orr.at[a], ssem.at[a, OOUT])
    wait_bytes(uo.at[pl.ds(0, 3 * CH)], ssem.at[1, OZ])
    wait_bytes(uo.at[pl.ds(0, 28 * CH)], ssem.at[1, OX])
    wait_bytes(gr1, ssem.at[1, G1])
    wait_bytes(gr2, ssem.at[1, G2])
    wait_bytes(gr1, ssem.at[1, G3])


def body(vectors, tiles, tile_rows, tile_cols):
    vmem = pl.BlockSpec(memory_space=pltpu.VMEM)
    smem = pl.BlockSpec(memory_space=pltpu.SMEM)
    hbm = pl.BlockSpec(memory_space=pltpu.HBM)
    return pl.pallas_call(
        kernel,
        out_shape=(
            jax.ShapeDtypeStruct((CH, V), BF),
            jax.ShapeDtypeStruct((CH, V), BF),
            jax.ShapeDtypeStruct((V, V), F32),
            jax.ShapeDtypeStruct((V, V), F32),
        ),
        in_specs=[hbm, hbm, smem, smem],
        out_specs=(vmem,) * 4,
        scratch_shapes=[
            pltpu.VMEM((GROUP, V), BF),
            pltpu.VMEM((K, TS, TS), BF),
            pltpu.VMEM((2, K, TS, TS), BF),
            pltpu.VMEM((GROUP, V), BF),
            pltpu.VMEM((GROUP, V), BF),
            pltpu.VMEM((GROUP, V), BF),
            pltpu.VMEM((K, TS, V), F32),
            pltpu.VMEM((2, GROUP, V), BF),
            pltpu.VMEM((2, GROUP, V), BF),
            pltpu.VMEM((2, 4, 7, CH, V), BF),
            pltpu.VMEM((2, 4, 7, CH, V), BF),
            pltpu.VMEM((2, 4, 2, CH, V), BF),
            pltpu.VMEM((2, 8, CH, V), BF),
            pltpu.VMEM((2, 4, CH, V), F32),
            pltpu.VMEM((2, 3, CH, V), F32),
            pltpu.VMEM((CH, V), BF),
            pltpu.VMEM((2 * V, V), F32),
            pltpu.VMEM((NCOL - 1, 8, V), F32),
            pltpu.VMEM((8, V), F32),
            pltpu.VMEM((G - 1, 8, V), F32),
            pltpu.VMEM((8, V), F32),
            pltpu.VMEM((2 * V, V), F32),
            pltpu.SemaphoreType.DMA((2, NSTAGE)),
            pltpu.SemaphoreType.DMA((2, NSTAGE, 8)),
            pltpu.SemaphoreType.DMA((2,)),
        ],
        compiler_params=pltpu.CompilerParams(
            collective_id=0, has_side_effects=True, vmem_limit_bytes=40 * 2**20
        ),
    )(vectors, tiles, tile_rows, tile_cols)


def solution(mesh):
    placed = (P("row", None), P(("row", "col"), None, None), P(("row", "col")), P(("row", "col")))
    return jax.shard_map(
        body,
        mesh=mesh,
        in_specs=placed,
        out_specs=(P(("row", "col"), None), P(("row", "col"), None), P(), P()),
        check_vma=False,
    )
```

```python
import jax
import jax.numpy as jnp
from jax import lax
from jax.experimental import pallas as pl
from jax.experimental.pallas import tpu as pltpu
from jax.sharding import PartitionSpec as P

MESH = pl.DeviceIdType.MESH
BF = jnp.bfloat16
F32 = jnp.float32
TS = 256
V = 128
NB = 12
G = 16
NCOL = 32
K = 8
GROUP = NB * TS
CH = GROUP // NCOL
QU = GROUP // 4
NROWS = GROUP * G

ZIN, YIN, YRS, ZOUT, OZ, OX, XRS, OOUT, G1, G2, G3 = range(11)
NSTAGE = 11


def loop(n, body):
    def step(i, carry):
        body(i)
        return carry

    lax.fori_loop(0, n, step, 0)


def kernel(
    vec_in, tiles_in, trows, tcols, out1, out2, gn, gr,
    vec, tiles, tt, up0, up1, uo, prod, pb, ob, yr, xr, zs, zr, osum, orr, ach,
    gs, gr1, gp, gr2, gf, ga, ssem, rsem, lsem,
):
    up = (up0, up1)
    r = lax.axis_index("row")
    c = lax.axis_index("col")
    y, zh = r // 4, r % 4
    zl, xk = c // 8, c % 8
    x, k = xk // 2, c % 2
    x1 = x + 1 - 2 * (x % 2)
    par = zl % 2
    p = c % G
    p1 = 8 * par + 2 * x1 + k
    is_high = p <= r
    to_xk = 2 * ((x + 2 * (y // 2)) % 4) + y % 2
    self_z = jnp.logical_and(p == r, y == zl)
    self_out = jnp.logical_and(jnp.logical_or(p == r, p1 == r), to_xk == xk)

    load_vec = pltpu.make_async_copy(vec_in, vec, lsem.at[0])
    load_tiles = pltpu.make_async_copy(tiles_in, tiles, lsem.at[1])
    load_vec.start()
    load_tiles.start()

    def wait_bytes(ref, sem):
        pltpu.make_async_copy(ref, ref, sem).wait()

    def z_group(i):
        j = i // 2
        return 4 * zl + (zh + 2 - j + 3 * (j // 2) - 2 * (j // 3)) % 4, r + G * (i % 2)

    def z_owner(i):
        return p, 8 * y + i

    def out_owner(q, e):
        return (p if e == 0 else p1), 8 * q + to_xk

    rx, rk, rpar = (r // 2) % 4, r % 2, r // 8
    flip = (x % 2 + rx % 2) % 2
    from_y = 2 * ((x // 2 + rx // 2) % 2) + k
    from_x = rx + flip * (1 - 2 * (rx % 2))

    def out_source(i):
        return 4 * from_y + i // 2, 8 * (rpar + 2 * (i % 2)) + 2 * from_x + rk

    def pair_mate(j):
        return 4 * j + zh, 8 * zl + 2 * x1 + k

    level, line = 8 * y + xk, 4 * zh + zl

    def level_mate(i):
        to = (level + i + 1) % 32
        return to, 4 * (to // 8) + zh, 8 * zl + to % 8

    def line_mate(i):
        to = (line + i + 1) % 16
        return 4 * y + to // 4, 8 * (to % 4) + xk

    barrier = pltpu.get_barrier_semaphore()

    def greet(row, col):
        pl.semaphore_signal(barrier, inc=1, device_id=(row, col), device_id_type=MESH)

    def greet_other(row, col):
        @pl.when(jnp.logical_or(row != r, col != c))
        def _():
            greet(row, col)

    loop(8, lambda i: greet_other(*z_group(i)))
    loop(8, lambda i: greet_other(*z_owner(i)))
    loop(4, lambda q: greet_other(*out_owner(q, 0)))
    loop(4, lambda q: greet_other(*out_owner(q, 1)))
    loop(8, lambda i: greet_other(*out_source(i)))
    loop(15, lambda i: greet(*line_mate(i)))
    loop(31, lambda i: greet(*level_mate(i)[1:]))

    straight = jnp.where(is_high, 0, 1)
    load_vec.wait()
    load_tiles.wait()

    def turn(k):
        t = tiles[k]
        tt[straight, k] = t
        tt[1 - straight, k] = t.T

    loop(K, turn)

    def within(block):
        return jnp.minimum(jnp.maximum(block, 0), NB - 1)

    def own_id(k):
        return within(jnp.where(is_high, trows[k], tcols[k]) - r * NB)

    def par_id(k):
        return within(jnp.where(is_high, tcols[k], trows[k]) - p * NB)

    def send(src, dst, a, stage, sub, row, col):
        pltpu.make_async_remote_copy(
            src_ref=src,
            dst_ref=dst,
            send_sem=ssem.at[a, stage],
            recv_sem=rsem.at[a, stage, sub],
            device_id=(row, col),
            device_id_type=MESH,
        ).start()

    def send_or_copy(src, dst, a, stage, sub, row, col):
        same = jnp.logical_and(row == r, col == c)

        @pl.when(same)
        def _():
            pltpu.make_async_copy(src, dst, rsem.at[a, stage, sub]).start()

        @pl.when(jnp.logical_not(same))
        def _():
            send(src, dst, a, stage, sub, row, col)

    def chunk(ref, i):
        return ref.at[pl.ds(pl.multiple_of(i * CH, CH), CH)]

    def read(ref, a, i):
        return ref[a, pl.ds(pl.multiple_of(i * CH, CH), CH), :].astype(F32)

    def z_in(a, src):
        loop(8, lambda i: send_or_copy(src, chunk(up[a], c), a, ZIN, xk, *z_group(i)))

    def y_in(a, first, count):
        def forward(i):
            part = chunk(up[a], 8 * y + first + i)
            wait_bytes(part, rsem.at[a, ZIN, first + i])
            loop(3, lambda j: send(part, part, a, YIN, 0, 4 * ((y + j + 1) % 4) + zh, c))

        loop(count, forward)

    def to_mates(src, where):
        loop(7, lambda i: send(src, chunk(uo, where), 1, OX, 0, r, 8 * zl + (xk + i + 1) % 8))

    def own_in():
        loop(3, lambda i: send(ach, chunk(uo, c), 1, OZ, i, r, 8 * ((zl + i + 1) % 4) + xk))
        to_mates(ach, c)

        def forward(i):
            cc = 8 * ((zl + 3 - i) % 4) + xk
            part = chunk(uo, cc)
            wait_bytes(part, rsem.at[1, OZ, i])
            to_mates(part, cc)

        loop(3, forward)

    def one_if_same(left, right):
        gap = left - right
        return (1 - jnp.minimum(gap * gap, 1)).astype(F32)

    def multiply(side, ids_from, source):
        def one(k):
            block = source[pl.ds(ids_from(k) * TS, TS), :]
            prod[k] = jnp.dot(tt[side, k], block, preferred_element_type=F32)

        loop(K, one)

    def gather(ids_to, target, a, q):
        def block(i):
            b = 3 * q + i
            weights = [one_if_same(ids_to(k), b) for k in range(K)]
            for s in range(4):
                piece = pl.ds(64 * s, 64)
                acc = prod[0, piece, :] * weights[0]
                for k in range(1, K):
                    acc = acc + prod[k, piece, :] * weights[k]
                target[a, pl.ds(pl.multiple_of(b * TS + 64 * s, 64), 64), :] = acc.astype(BF)

        loop(3, block)

    def y_out(a, q):
        def mate(i):
            j = (y + i + 1) % 4
            part = chunk(pb.at[a], 8 * q + 2 * ((x + 2 * (j // 2)) % 4) + j % 2)
            send(part, yr.at[a, q, i], a, YRS, q, 4 * j + zh, c)

        def pair(i):
            j = (y + i) % 4
            part = chunk(pb.at[a], 8 * q + 2 * ((x1 + 2 * (j // 2)) % 4) + j % 2)
            send(part, yr.at[a, q, 3 + i], a, YRS, q, *pair_mate(j))

        loop(4, pair)
        loop(3, mate)

    def z_out(a, q):
        slot = zh * 2 + c // G
        wait_bytes(yr.at[a, q], rsem.at[a, YRS, q])
        acc = read(pb, a, 8 * q + to_xk)
        for i in range(3):
            acc = acc + yr[a, q, i].astype(F32)
        zs[a, q, 0] = acc.astype(BF)
        acc = yr[a, q, 3].astype(F32)
        for i in range(4, 7):
            acc = acc + yr[a, q, i].astype(F32)
        zs[a, q, 1] = acc.astype(BF)
        send_or_copy(zs.at[a, q, 0], zr.at[a, slot], a, ZOUT, 0, *out_owner(q, 0))
        send_or_copy(zs.at[a, q, 1], zr.at[a, slot], a, ZOUT, 0, *out_owner(q, 1))

    def x_out(a, q):
        def mate(i):
            to = (xk + i + 1) % 8
            send(chunk(ob.at[a], 8 * q + to), xr.at[a, q, i], a, XRS, q, r, 8 * zl + to)

        loop(7, mate)

    def own_sum(a, q):
        wait_bytes(xr.at[a, q], rsem.at[a, XRS, q])
        acc = read(ob, a, 8 * q + xk)
        for i in range(7):
            acc = acc + xr[a, q, i].astype(F32)
        osum[a, q] = acc

    def own_out(a):
        def step(i):
            q = (zl + i + 1) % 4
            own_sum(a, q)
            send(osum.at[a, q], orr.at[a, i], a, OOUT, 0, r, 8 * q + xk)

        loop(3, step)
        own_sum(a, zl)

    def total(a):
        wait_bytes(orr.at[a], rsem.at[a, OOUT, 0])
        wait_bytes(zr.at[a], rsem.at[a, ZOUT, 0])
        acc = osum[a, zl]
        for i in range(3):
            acc = acc + orr[a, i]
        for i in range(8):
            acc = acc + zr[a, i].astype(F32)
        return acc.astype(BF)

    def inner(left, right):
        return lax.dot_general(left, right, (((0,), (0,)), ((), ())), preferred_element_type=F32)

    multiply(1, own_id, vec)
    loop(4, lambda q: gather(par_id, pb, 0, q))
    waits = 31 + 15 + 32
    pl.semaphore_wait(
        barrier, waits - 2 * jnp.where(self_z, 1, 0) - 2 * jnp.where(self_out, 1, 0)
    )
    z_in(0, chunk(vec, c))
    loop(4, lambda q: y_out(0, q))
    loop(2, lambda q: z_out(0, q))
    y_in(0, 0, 2)
    z_out(0, 2)
    y_in(0, 2, 2)
    z_out(0, 3)
    y_in(0, 4, 4)
    wait_bytes(up[0].at[pl.ds(0, 3 * QU)], rsem.at[0, YIN, 0])
    multiply(0, par_id, up[0])

    def own_step(i):
        q = (zl + i + 1) % 4
        gather(own_id, ob, 0, q)
        x_out(0, q)

    loop(4, own_step)
    own_out(0)
    first = total(0)
    ach[...] = first

    z_in(1, ach)
    own_in()
    out1[...] = first
    uo[pl.ds(pl.multiple_of(c * CH, CH), CH), :] = first
    gs[pl.ds(0, V), :] = inner(first, first)
    y_in(1, 0, 8)
    wait_bytes(uo.at[pl.ds(0, 28 * CH)], rsem.at[1, OX, 0])
    multiply(1, own_id, uo)

    def partner_step(q):
        gather(par_id, pb, 1, q)
        y_out(1, q)

    loop(4, partner_step)
    wait_bytes(up[1].at[pl.ds(0, 3 * QU)], rsem.at[1, YIN, 0])

    gs[pl.ds(V, V), :] = inner(up[1][...], pb[1])

    def gram_out(i):
        to, row, col = level_mate(i)
        send(gs.at[pl.ds(pl.multiple_of(to * 8, 8), 8)], gr1.at[i], 1, G1, 0, row, col)

    loop(31, gram_out)
    multiply(0, par_id, up[1])

    def both_step(i):
        q = (zl + i + 1) % 4
        gather(own_id, ob, 1, q)
        x_out(1, q)
        z_out(1, i)

    loop(4, both_step)

    wait_bytes(gr1, rsem.at[1, G1, 0])
    mine = pl.ds(pl.multiple_of(level * 8, 8), 8)
    gp[...] = lax.fori_loop(0, 31, lambda i, s: s + gr1[i], gs[mine, :])
    loop(15, lambda i: send(gp, gr2.at[i], 1, G2, 0, *line_mate(i)))
    own_out(1)
    wait_bytes(gr2, rsem.at[1, G2, 0])
    acc = lax.fori_loop(0, 15, lambda i, s: s + gr2[i], gp[...])
    gf[...] = acc
    loop(31, lambda i: send(gf, ga.at[mine], 1, G3, 0, *level_mate(i)[1:]))
    ga[mine, :] = acc
    out2[...] = total(1)
    wait_bytes(ga.at[pl.ds(0, 2 * V - 8)], rsem.at[1, G3, 0])
    gn[...] = ga[pl.ds(0, V), :] / NROWS
    half = ga[pl.ds(V, V), :]
    gr[...] = (half + half.T) / NROWS

    def sent(a, stage, less, chunks):
        @pl.when(less)
        def _():
            wait_bytes(up[a].at[pl.ds(0, (chunks - 1) * CH)], ssem.at[a, stage])

        @pl.when(jnp.logical_not(less))
        def _():
            wait_bytes(up[a].at[pl.ds(0, chunks * CH)], ssem.at[a, stage])

    for a in range(2):
        sent(a, ZIN, self_z, 8)
        sent(a, ZOUT, self_out, 8)
        wait_bytes(up[a].at[pl.ds(0, 24 * CH)], ssem.at[a, YIN])
        wait_bytes(yr.at[a], ssem.at[a, YRS])
        wait_bytes(xr.at[a], ssem.at[a, XRS])
        wait_bytes(orr.at[a], ssem.at[a, OOUT])
    wait_bytes(uo.at[pl.ds(0, 3 * CH)], ssem.at[1, OZ])
    wait_bytes(uo.at[pl.ds(0, 28 * CH)], ssem.at[1, OX])
    wait_bytes(gr1, ssem.at[1, G1])
    wait_bytes(gr2, ssem.at[1, G2])
    wait_bytes(gr1, ssem.at[1, G3])


def body(vectors, tiles, tile_rows, tile_cols):
    vmem = pl.BlockSpec(memory_space=pltpu.VMEM)
    smem = pl.BlockSpec(memory_space=pltpu.SMEM)
    hbm = pl.BlockSpec(memory_space=pltpu.HBM)
    return pl.pallas_call(
        kernel,
        out_shape=(
            jax.ShapeDtypeStruct((CH, V), BF),
            jax.ShapeDtypeStruct((CH, V), BF),
            jax.ShapeDtypeStruct((V, V), F32),
            jax.ShapeDtypeStruct((V, V), F32),
        ),
        in_specs=[hbm, hbm, smem, smem],
        out_specs=(vmem,) * 4,
        scratch_shapes=[
            pltpu.VMEM((GROUP, V), BF),
            pltpu.VMEM((K, TS, TS), BF),
            pltpu.VMEM((2, K, TS, TS), BF),
            pltpu.VMEM((GROUP, V), BF),
            pltpu.VMEM((GROUP, V), BF),
            pltpu.VMEM((GROUP, V), BF),
            pltpu.VMEM((K, TS, V), F32),
            pltpu.VMEM((2, GROUP, V), BF),
            pltpu.VMEM((2, GROUP, V), BF),
            pltpu.VMEM((2, 4, 7, CH, V), BF),
            pltpu.VMEM((2, 4, 7, CH, V), BF),
            pltpu.VMEM((2, 4, 2, CH, V), BF),
            pltpu.VMEM((2, 8, CH, V), BF),
            pltpu.VMEM((2, 4, CH, V), F32),
            pltpu.VMEM((2, 3, CH, V), F32),
            pltpu.VMEM((CH, V), BF),
            pltpu.VMEM((2 * V, V), F32),
            pltpu.VMEM((NCOL - 1, 8, V), F32),
            pltpu.VMEM((8, V), F32),
            pltpu.VMEM((G - 1, 8, V), F32),
            pltpu.VMEM((8, V), F32),
            pltpu.VMEM((2 * V, V), F32),
            pltpu.SemaphoreType.DMA((2, NSTAGE)),
            pltpu.SemaphoreType.DMA((2, NSTAGE, 8)),
            pltpu.SemaphoreType.DMA((2,)),
        ],
        compiler_params=pltpu.CompilerParams(
            collective_id=0, has_side_effects=True, vmem_limit_bytes=64 * 2**20
        ),
    )(vectors, tiles, tile_rows, tile_cols)


def solution(mesh):
    placed = (P("row", None), P(("row", "col"), None, None), P(("row", "col")), P(("row", "col")))
    return jax.shard_map(
        body,
        mesh=mesh,
        in_specs=placed,
        out_specs=(P(("row", "col"), None), P(("row", "col"), None), P(), P()),
        check_vma=False,
    )
```

```python
import jax
import jax.numpy as jnp
from jax import lax
from jax.experimental import pallas as pl
from jax.experimental.pallas import tpu as pltpu
from jax.sharding import PartitionSpec as P

MESH = pl.DeviceIdType.MESH
BF = jnp.bfloat16
F32 = jnp.float32
TS = 256
V = 128
NB = 12
G = 16
NCOL = 32
K = 8
GROUP = NB * TS
CH = GROUP // NCOL
QU = GROUP // 4
NROWS = GROUP * G

ZIN, YIN, YRS, ZOUT, OZ, OX, SIB, XRS, OOUT, G1, G2, G3 = range(12)
NSTAGE = 12


def loop(n, body):
    def step(i, carry):
        body(i)
        return carry

    lax.fori_loop(0, n, step, 0)


def kernel(
    vec_in, tiles_in, trows, tcols, out1, out2, gn, gr,
    vec, tiles, tt, up0, up1, uo, prod, pb, ob, yr, sib, xs, xr, zs, zr, osum, orr, ach,
    gs, gr1, gp, gr2, gf, ga, ssem, rsem, lsem,
):
    up = (up0, up1)
    r = lax.axis_index("row")
    c = lax.axis_index("col")
    y, zh = r // 4, r % 4
    zl, xk = c // 8, c % 8
    x, k = xk // 2, c % 2
    x1 = x + 1 - 2 * (x % 2)
    par = zl % 2
    p = c % G
    p1 = 8 * par + 2 * x1 + k
    is_high = p <= r
    to_xk = 2 * ((x + 2 * (y // 2)) % 4) + y % 2
    self_z = jnp.logical_and(p == r, y == zl)
    self_out = jnp.logical_and(jnp.logical_or(p == r, p1 == r), to_xk == xk)

    load_vec = pltpu.make_async_copy(vec_in, vec, lsem.at[0])
    load_tiles = pltpu.make_async_copy(tiles_in, tiles, lsem.at[1])
    load_vec.start()
    load_tiles.start()

    def wait_bytes(ref, sem):
        pltpu.make_async_copy(ref, ref, sem).wait()

    def z_group(i):
        j = i // 2
        return 4 * zl + (zh + 2 - j + 3 * (j // 2) - 2 * (j // 3)) % 4, r + G * (i % 2)

    def z_owner(i):
        return p, 8 * y + i

    def out_owner(q, e):
        return (p if e == 0 else p1), 8 * q + to_xk

    rx, rk, rpar = (r // 2) % 4, r % 2, r // 8
    flip = (x % 2 + rx % 2) % 2
    from_y = 2 * ((x // 2 + rx // 2) % 2) + k
    from_x = rx + flip * (1 - 2 * (rx % 2))

    def out_source(i):
        return 4 * from_y + i // 2, 8 * (rpar + 2 * (i % 2)) + 2 * from_x + rk

    def pair_mate(j):
        return 4 * j + zh, 8 * zl + 2 * x1 + k

    level, line = 8 * y + xk, 4 * zh + zl

    def level_mate(i):
        to = (level + i + 1) % 32
        return to, 4 * (to // 8) + zh, 8 * zl + to % 8

    def line_mate(i):
        to = (line + i + 1) % 16
        return 4 * y + to // 4, 8 * (to % 4) + xk

    barrier = pltpu.get_barrier_semaphore()

    def greet(row, col):
        pl.semaphore_signal(barrier, inc=1, device_id=(row, col), device_id_type=MESH)

    def greet_other(row, col):
        @pl.when(jnp.logical_or(row != r, col != c))
        def _():
            greet(row, col)

    loop(8, lambda i: greet_other(*z_group(i)))
    loop(8, lambda i: greet_other(*z_owner(i)))
    loop(4, lambda q: greet_other(*out_owner(q, 0)))
    loop(4, lambda q: greet_other(*out_owner(q, 1)))
    loop(8, lambda i: greet_other(*out_source(i)))
    loop(15, lambda i: greet(*line_mate(i)))
    loop(31, lambda i: greet(*level_mate(i)[1:]))

    straight = jnp.where(is_high, 0, 1)
    load_vec.wait()
    load_tiles.wait()

    def turn(k):
        t = tiles[k]
        tt[straight, k] = t
        tt[1 - straight, k] = t.T

    loop(K, turn)

    def within(block):
        return jnp.minimum(jnp.maximum(block, 0), NB - 1)

    def own_id(k):
        return within(jnp.where(is_high, trows[k], tcols[k]) - r * NB)

    def par_id(k):
        return within(jnp.where(is_high, tcols[k], trows[k]) - p * NB)

    def send(src, dst, a, stage, sub, row, col):
        pltpu.make_async_remote_copy(
            src_ref=src,
            dst_ref=dst,
            send_sem=ssem.at[a, stage],
            recv_sem=rsem.at[a, stage, sub],
            device_id=(row, col),
            device_id_type=MESH,
        ).start()

    def send_or_copy(src, dst, a, stage, sub, row, col):
        same = jnp.logical_and(row == r, col == c)

        @pl.when(same)
        def _():
            pltpu.make_async_copy(src, dst, rsem.at[a, stage, sub]).start()

        @pl.when(jnp.logical_not(same))
        def _():
            send(src, dst, a, stage, sub, row, col)

    def chunk(ref, i):
        return ref.at[pl.ds(pl.multiple_of(i * CH, CH), CH)]

    def read(ref, a, i):
        return ref[a, pl.ds(pl.multiple_of(i * CH, CH), CH), :].astype(F32)

    def z_in(a, src):
        loop(8, lambda i: send_or_copy(src, chunk(up[a], c), a, ZIN, xk, *z_group(i)))

    def y_in(a, first, count):
        def forward(i):
            part = chunk(up[a], 8 * y + first + i)
            wait_bytes(part, rsem.at[a, ZIN, first + i])
            loop(3, lambda j: send(part, part, a, YIN, 0, 4 * ((y + j + 1) % 4) + zh, c))

        loop(count, forward)

    def to_mates(src, where):
        loop(7, lambda i: send(src, chunk(uo, where), 1, OX, 0, r, 8 * zl + (xk + i + 1) % 8))

    def own_in():
        loop(3, lambda i: send(ach, chunk(uo, c), 1, OZ, i, r, 8 * ((zl + i + 1) % 4) + xk))
        to_mates(ach, c)

        def forward(i):
            cc = 8 * ((zl + 3 - i) % 4) + xk
            part = chunk(uo, cc)
            wait_bytes(part, rsem.at[1, OZ, i])
            to_mates(part, cc)

        loop(3, forward)

    def one_if_same(left, right):
        gap = left - right
        return (1 - jnp.minimum(gap * gap, 1)).astype(F32)

    def multiply(side, ids_from, source):
        def one(k):
            block = source[pl.ds(ids_from(k) * TS, TS), :]
            prod[k] = jnp.dot(tt[side, k], block, preferred_element_type=F32)

        loop(K, one)

    def gather(ids_to, target, a, q):
        def block(i):
            b = 3 * q + i
            weights = [one_if_same(ids_to(k), b) for k in range(K)]
            for s in range(4):
                piece = pl.ds(64 * s, 64)
                acc = prod[0, piece, :] * weights[0]
                for k in range(1, K):
                    acc = acc + prod[k, piece, :] * weights[k]
                target[a, pl.ds(pl.multiple_of(b * TS + 64 * s, 64), 64), :] = acc.astype(target.dtype)

        loop(3, block)

    def y_out(a, q):
        def mate(i):
            j = (y + i + 1) % 4
            part = chunk(pb.at[a], 8 * q + 2 * ((x + 2 * (j // 2)) % 4) + j % 2)
            send(part, yr.at[a, q, i], a, YRS, q, 4 * j + zh, c)

        def pair(i):
            j = (y + i) % 4
            part = chunk(pb.at[a], 8 * q + 2 * ((x1 + 2 * (j // 2)) % 4) + j % 2)
            send(part, yr.at[a, q, 3 + i], a, YRS, q, *pair_mate(j))

        loop(4, pair)
        loop(3, mate)

    def z_out(a, q):
        slot = zh * 2 + c // G
        wait_bytes(yr.at[a, q], rsem.at[a, YRS, q])
        acc = read(pb, a, 8 * q + to_xk)
        for i in range(3):
            acc = acc + yr[a, q, i].astype(F32)
        zs[a, q, 0] = acc.astype(BF)
        acc = yr[a, q, 3].astype(F32)
        for i in range(4, 7):
            acc = acc + yr[a, q, i].astype(F32)
        zs[a, q, 1] = acc.astype(BF)
        send_or_copy(zs.at[a, q, 0], zr.at[a, slot], a, ZOUT, 0, *out_owner(q, 0))
        send_or_copy(zs.at[a, q, 1], zr.at[a, slot], a, ZOUT, 0, *out_owner(q, 1))

    def pair_out(a, q):
        def piece(i):
            part = chunk(ob.at[a], 8 * q + 2 * i + 1 - k)
            send(part, sib.at[a, q, i], a, SIB, q, r, 8 * zl + 2 * x + 1 - k)

        loop(4, piece)

    def x_out(a, q):
        wait_bytes(sib.at[a, q], rsem.at[a, SIB, q])

        def mate(i):
            to = (x + i + 1) % 4
            xs[a, q, i] = (read(ob, a, 8 * q + 2 * to + k) + sib[a, q, to]).astype(BF)
            send(xs.at[a, q, i], xr.at[a, q, i], a, XRS, q, r, 8 * zl + 2 * to + k)

        loop(3, mate)

    def own_sum(a, q):
        acc = read(ob, a, 8 * q + xk) + sib[a, q, x]
        wait_bytes(xr.at[a, q], rsem.at[a, XRS, q])
        for i in range(3):
            acc = acc + xr[a, q, i].astype(F32)
        osum[a, q] = acc

    def own_out(a):
        def step(i):
            q = (zl + i + 1) % 4
            own_sum(a, q)
            send(osum.at[a, q], orr.at[a, i], a, OOUT, 0, r, 8 * q + xk)

        loop(3, step)
        own_sum(a, zl)

    def total(a):
        wait_bytes(orr.at[a], rsem.at[a, OOUT, 0])
        wait_bytes(zr.at[a], rsem.at[a, ZOUT, 0])
        acc = osum[a, zl]
        for i in range(3):
            acc = acc + orr[a, i]
        for i in range(8):
            acc = acc + zr[a, i].astype(F32)
        return acc.astype(BF)

    def inner(left, right):
        return lax.dot_general(left, right, (((0,), (0,)), ((), ())), preferred_element_type=F32)

    multiply(1, own_id, vec)
    loop(4, lambda q: gather(par_id, pb, 0, q))
    waits = 31 + 15 + 32
    pl.semaphore_wait(
        barrier, waits - 2 * jnp.where(self_z, 1, 0) - 2 * jnp.where(self_out, 1, 0)
    )
    z_in(0, chunk(vec, c))
    loop(4, lambda q: y_out(0, q))
    loop(2, lambda q: z_out(0, q))
    y_in(0, 0, 2)
    z_out(0, 2)
    y_in(0, 2, 2)
    z_out(0, 3)
    y_in(0, 4, 4)
    wait_bytes(up[0].at[pl.ds(0, 3 * QU)], rsem.at[0, YIN, 0])
    multiply(0, par_id, up[0])

    def nth(i):
        return (zl + i + 1) % 4

    def own_gather(a, i):
        gather(own_id, ob, a, nth(i))
        pair_out(a, nth(i))

    def own_products(a):
        own_gather(a, 0)

        def step(i):
            own_gather(a, i + 1)
            x_out(a, nth(i))

        loop(3, step)
        x_out(a, nth(3))

    own_products(0)
    own_out(0)
    first = total(0)
    ach[...] = first

    z_in(1, ach)
    own_in()
    out1[...] = first
    uo[pl.ds(pl.multiple_of(c * CH, CH), CH), :] = first
    gs[pl.ds(0, V), :] = inner(first, first)
    y_in(1, 0, 8)
    wait_bytes(uo.at[pl.ds(0, 28 * CH)], rsem.at[1, OX, 0])
    multiply(1, own_id, uo)

    def partner_step(q):
        gather(par_id, pb, 1, q)
        y_out(1, q)

    loop(4, partner_step)
    wait_bytes(up[1].at[pl.ds(0, 3 * QU)], rsem.at[1, YIN, 0])

    gs[pl.ds(V, V), :] = inner(up[1][...], pb[1])

    def gram_out(i):
        to, row, col = level_mate(i)
        send(gs.at[pl.ds(pl.multiple_of(to * 8, 8), 8)], gr1.at[i], 1, G1, 0, row, col)

    loop(31, gram_out)
    multiply(0, par_id, up[1])

    own_products(1)
    wait_bytes(gr1, rsem.at[1, G1, 0])
    mine = pl.ds(pl.multiple_of(level * 8, 8), 8)
    gp[...] = lax.fori_loop(0, 31, lambda i, s: s + gr1[i], gs[mine, :])
    loop(15, lambda i: send(gp, gr2.at[i], 1, G2, 0, *line_mate(i)))
    loop(4, lambda q: z_out(1, q))
    own_out(1)
    wait_bytes(gr2, rsem.at[1, G2, 0])
    acc = lax.fori_loop(0, 15, lambda i, s: s + gr2[i], gp[...])
    gf[...] = acc
    loop(31, lambda i: send(gf, ga.at[mine], 1, G3, 0, *level_mate(i)[1:]))
    ga[mine, :] = acc
    out2[...] = total(1)
    wait_bytes(ga.at[pl.ds(0, 2 * V - 8)], rsem.at[1, G3, 0])
    gn[...] = ga[pl.ds(0, V), :] / NROWS
    half = ga[pl.ds(V, V), :]
    gr[...] = (half + half.T) / NROWS

    def sent(a, stage, less, chunks):
        @pl.when(less)
        def _():
            wait_bytes(up[a].at[pl.ds(0, (chunks - 1) * CH)], ssem.at[a, stage])

        @pl.when(jnp.logical_not(less))
        def _():
            wait_bytes(up[a].at[pl.ds(0, chunks * CH)], ssem.at[a, stage])

    for a in range(2):
        sent(a, ZIN, self_z, 8)
        sent(a, ZOUT, self_out, 8)
        wait_bytes(up[a].at[pl.ds(0, 24 * CH)], ssem.at[a, YIN])
        wait_bytes(yr.at[a], ssem.at[a, YRS])
        wait_bytes(sib.at[a], ssem.at[a, SIB])
        wait_bytes(xr.at[a], ssem.at[a, XRS])
        wait_bytes(orr.at[a], ssem.at[a, OOUT])
    wait_bytes(uo.at[pl.ds(0, 3 * CH)], ssem.at[1, OZ])
    wait_bytes(uo.at[pl.ds(0, 28 * CH)], ssem.at[1, OX])
    wait_bytes(gr1, ssem.at[1, G1])
    wait_bytes(gr2, ssem.at[1, G2])
    wait_bytes(gr1, ssem.at[1, G3])


def hand_over(*refs):
    for i in range(4):
        refs[4 + i][...] = refs[i][...]


def body(vectors, tiles, tile_rows, tile_cols):
    vmem = pl.BlockSpec(memory_space=pltpu.VMEM)
    smem = pl.BlockSpec(memory_space=pltpu.SMEM)
    hbm = pl.BlockSpec(memory_space=pltpu.HBM)
    outs = (
        jax.ShapeDtypeStruct((CH, V), BF),
        jax.ShapeDtypeStruct((CH, V), BF),
        jax.ShapeDtypeStruct((V, V), F32),
        jax.ShapeDtypeStruct((V, V), F32),
    )
    results = pl.pallas_call(
        kernel,
        out_shape=outs,
        in_specs=[hbm, hbm, smem, smem],
        out_specs=(vmem,) * 4,
        scratch_shapes=[
            pltpu.VMEM((GROUP, V), BF),
            pltpu.VMEM((K, TS, TS), BF),
            pltpu.VMEM((2, K, TS, TS), BF),
            pltpu.VMEM((GROUP, V), BF),
            pltpu.VMEM((GROUP, V), BF),
            pltpu.VMEM((GROUP, V), BF),
            pltpu.VMEM((K, TS, V), F32),
            pltpu.VMEM((2, GROUP, V), BF),
            pltpu.VMEM((2, GROUP, V), F32),
            pltpu.VMEM((2, 4, 7, CH, V), BF),
            pltpu.VMEM((2, 4, 4, CH, V), F32),
            pltpu.VMEM((2, 4, 3, CH, V), BF),
            pltpu.VMEM((2, 4, 3, CH, V), BF),
            pltpu.VMEM((2, 4, 2, CH, V), BF),
            pltpu.VMEM((2, 8, CH, V), BF),
            pltpu.VMEM((2, 4, CH, V), F32),
            pltpu.VMEM((2, 3, CH, V), F32),
            pltpu.VMEM((CH, V), BF),
            pltpu.VMEM((2 * V, V), F32),
            pltpu.VMEM((NCOL - 1, 8, V), F32),
            pltpu.VMEM((8, V), F32),
            pltpu.VMEM((G - 1, 8, V), F32),
            pltpu.VMEM((8, V), F32),
            pltpu.VMEM((2 * V, V), F32),
            pltpu.SemaphoreType.DMA((2, NSTAGE)),
            pltpu.SemaphoreType.DMA((2, NSTAGE, 8)),
            pltpu.SemaphoreType.DMA((2,)),
        ],
        compiler_params=pltpu.CompilerParams(
            collective_id=0, has_side_effects=True, vmem_limit_bytes=64 * 2**20
        ),
    )(vectors, tiles, tile_rows, tile_cols)
    return pl.pallas_call(
        hand_over,
        out_shape=outs,
        in_specs=[vmem] * 4,
        out_specs=(vmem,) * 4,
        compiler_params=pltpu.CompilerParams(vmem_limit_bytes=64 * 2**20),
    )(*results)


def solution(mesh):
    placed = (P("row", None), P(("row", "col"), None, None), P(("row", "col")), P(("row", "col")))
    return jax.shard_map(
        body,
        mesh=mesh,
        in_specs=placed,
        out_specs=(P(("row", "col"), None), P(("row", "col"), None), P(), P()),
        check_vma=False,
    )
```

```python
import jax
import jax.numpy as jnp
from jax import lax
from jax.experimental import pallas as pl
from jax.experimental.pallas import tpu as pltpu
from jax.sharding import PartitionSpec as P

MESH = pl.DeviceIdType.MESH
BF = jnp.bfloat16
F32 = jnp.float32
TS = 256
V = 128
NB = 12
G = 16
NCOL = 32
K = 8
GROUP = NB * TS
CH = GROUP // NCOL
QU = GROUP // 4
NROWS = GROUP * G

ZIN, YIN, YRS, ZOUT, OZ, OX, SIB, XRS, OOUT, G1, G2, G3 = range(12)
NSTAGE = 12


def loop(n, body):
    def step(i, carry):
        body(i)
        return carry

    lax.fori_loop(0, n, step, 0)


def kernel(
    vec_in, tiles_in, trows, tcols, out1, out2, gn, gr,
    vec, tiles, tt, up0, up1, uo, prod, pb, ob, yr, sib, xs, xr, zs, zr, osum, orr, ach,
    gs, gr1, gp, gr2, gf, ga, ssem, rsem, lsem,
):
    up = (up0, up1)
    r = lax.axis_index("row")
    c = lax.axis_index("col")
    y, zh = r // 4, r % 4
    zl, xk = c // 8, c % 8
    x, k = xk // 2, c % 2
    x1 = x + 1 - 2 * (x % 2)
    par = zl % 2
    p = c % G
    p1 = 8 * par + 2 * x1 + k
    is_high = p <= r
    to_xk = 2 * ((x + 2 * (y // 2)) % 4) + y % 2
    self_z = jnp.logical_and(p == r, y == zl)
    self_out = jnp.logical_and(jnp.logical_or(p == r, p1 == r), to_xk == xk)

    load_vec = pltpu.make_async_copy(vec_in, vec, lsem.at[0])
    load_tiles = pltpu.make_async_copy(tiles_in, tiles, lsem.at[1])
    load_vec.start()
    load_tiles.start()

    def wait_bytes(ref, sem):
        pltpu.make_async_copy(ref, ref, sem).wait()

    def z_group(i):
        j = i // 2
        return 4 * zl + (zh + 2 - j + 3 * (j // 2) - 2 * (j // 3)) % 4, r + G * (i % 2)

    def z_owner(i):
        return p, 8 * y + i

    def out_owner(q, e):
        return (p if e == 0 else p1), 8 * q + to_xk

    rx, rk, rpar = (r // 2) % 4, r % 2, r // 8
    flip = (x % 2 + rx % 2) % 2
    from_y = 2 * ((x // 2 + rx // 2) % 2) + k
    from_x = rx + flip * (1 - 2 * (rx % 2))

    def out_source(i):
        return 4 * from_y + i // 2, 8 * (rpar + 2 * (i % 2)) + 2 * from_x + rk

    def pair_mate(j):
        return 4 * j + zh, 8 * zl + 2 * x1 + k

    level, line = 8 * y + xk, 4 * zh + zl

    def level_mate(i):
        to = (level + i + 1) % 32
        return to, 4 * (to // 8) + zh, 8 * zl + to % 8

    def line_mate(i):
        to = (line + i + 1) % 16
        return 4 * y + to // 4, 8 * (to % 4) + xk

    barrier = pltpu.get_barrier_semaphore()

    def greet(row, col):
        pl.semaphore_signal(barrier, inc=1, device_id=(row, col), device_id_type=MESH)

    def greet_other(row, col):
        @pl.when(jnp.logical_or(row != r, col != c))
        def _():
            greet(row, col)

    loop(8, lambda i: greet_other(*z_group(i)))
    loop(8, lambda i: greet_other(*z_owner(i)))
    loop(4, lambda q: greet_other(*out_owner(q, 0)))
    loop(4, lambda q: greet_other(*out_owner(q, 1)))
    loop(8, lambda i: greet_other(*out_source(i)))
    loop(15, lambda i: greet(*line_mate(i)))
    loop(31, lambda i: greet(*level_mate(i)[1:]))

    straight = jnp.where(is_high, 0, 1)
    load_vec.wait()
    load_tiles.wait()

    def turn(k):
        t = tiles[k]
        tt[straight, k] = t
        tt[1 - straight, k] = t.T

    loop(K, turn)

    def within(block):
        return jnp.minimum(jnp.maximum(block, 0), NB - 1)

    def own_id(k):
        return within(jnp.where(is_high, trows[k], tcols[k]) - r * NB)

    def par_id(k):
        return within(jnp.where(is_high, tcols[k], trows[k]) - p * NB)

    def send(src, dst, a, stage, sub, row, col):
        pltpu.make_async_remote_copy(
            src_ref=src,
            dst_ref=dst,
            send_sem=ssem.at[a, stage],
            recv_sem=rsem.at[a, stage, sub],
            device_id=(row, col),
            device_id_type=MESH,
        ).start()

    def send_or_copy(src, dst, a, stage, sub, row, col):
        same = jnp.logical_and(row == r, col == c)

        @pl.when(same)
        def _():
            pltpu.make_async_copy(src, dst, rsem.at[a, stage, sub]).start()

        @pl.when(jnp.logical_not(same))
        def _():
            send(src, dst, a, stage, sub, row, col)

    def chunk(ref, i):
        return ref.at[pl.ds(pl.multiple_of(i * CH, CH), CH)]

    def read(ref, a, i):
        return ref[a, pl.ds(pl.multiple_of(i * CH, CH), CH), :].astype(F32)

    def z_in(a, src):
        loop(8, lambda i: send_or_copy(src, chunk(up[a], c), a, ZIN, xk, *z_group(i)))

    def y_in(a, first, count):
        def forward(i):
            part = chunk(up[a], 8 * y + first + i)
            wait_bytes(part, rsem.at[a, ZIN, first + i])
            loop(3, lambda j: send(part, part, a, YIN, 0, 4 * ((y + j + 1) % 4) + zh, c))

        loop(count, forward)

    def to_mates(src, where):
        loop(7, lambda i: send(src, chunk(uo, where), 1, OX, 0, r, 8 * zl + (xk + i + 1) % 8))

    def own_in():
        loop(3, lambda i: send(ach, chunk(uo, c), 1, OZ, i, r, 8 * ((zl + i + 1) % 4) + xk))
        to_mates(ach, c)

        def forward(i):
            cc = 8 * ((zl + 3 - i) % 4) + xk
            part = chunk(uo, cc)
            wait_bytes(part, rsem.at[1, OZ, i])
            to_mates(part, cc)

        loop(3, forward)

    def one_if_same(left, right):
        gap = left - right
        return (1 - jnp.minimum(gap * gap, 1)).astype(F32)

    def multiply(side, ids_from, source):
        def one(k):
            block = source[pl.ds(ids_from(k) * TS, TS), :]
            prod[k] = jnp.dot(tt[side, k], block, preferred_element_type=F32)

        loop(K, one)

    def gather(ids_to, target, a, q):
        def block(i):
            b = 3 * q + i
            weights = [one_if_same(ids_to(k), b) for k in range(K)]
            for s in range(4):
                piece = pl.ds(64 * s, 64)
                acc = prod[0, piece, :] * weights[0]
                for k in range(1, K):
                    acc = acc + prod[k, piece, :] * weights[k]
                target[a, pl.ds(pl.multiple_of(b * TS + 64 * s, 64), 64), :] = acc.astype(target.dtype)

        loop(3, block)

    def y_out(a, q):
        def mate(i):
            j = (y + i + 1) % 4
            part = chunk(pb.at[a], 8 * q + 2 * ((x + 2 * (j // 2)) % 4) + j % 2)
            send(part, yr.at[a, q, i], a, YRS, q, 4 * j + zh, c)

        def pair(i):
            j = (y + i) % 4
            part = chunk(pb.at[a], 8 * q + 2 * ((x1 + 2 * (j // 2)) % 4) + j % 2)
            send(part, yr.at[a, q, 3 + i], a, YRS, q, *pair_mate(j))

        loop(4, pair)
        loop(3, mate)

    def z_out(a, q):
        slot = zh * 2 + c // G
        wait_bytes(yr.at[a, q], rsem.at[a, YRS, q])
        acc = read(pb, a, 8 * q + to_xk)
        for i in range(3):
            acc = acc + yr[a, q, i].astype(F32)
        zs[a, q, 0] = acc.astype(BF)
        acc = yr[a, q, 3].astype(F32)
        for i in range(4, 7):
            acc = acc + yr[a, q, i].astype(F32)
        zs[a, q, 1] = acc.astype(BF)
        send_or_copy(zs.at[a, q, 0], zr.at[a, slot], a, ZOUT, 0, *out_owner(q, 0))
        send_or_copy(zs.at[a, q, 1], zr.at[a, slot], a, ZOUT, 0, *out_owner(q, 1))

    def pair_out(a, q):
        def piece(i):
            part = chunk(ob.at[a], 8 * q + 2 * i + 1 - k)
            send(part, sib.at[a, q, i], a, SIB, q, r, 8 * zl + 2 * x + 1 - k)

        loop(4, piece)

    def x_out(a, q):
        wait_bytes(sib.at[a, q], rsem.at[a, SIB, q])

        def mate(i):
            to = (x + i + 1) % 4
            xs[a, q, i] = (read(ob, a, 8 * q + 2 * to + k) + sib[a, q, to]).astype(BF)
            send(xs.at[a, q, i], xr.at[a, q, i], a, XRS, q, r, 8 * zl + 2 * to + k)

        loop(3, mate)

    def own_sum(a, q):
        acc = read(ob, a, 8 * q + xk) + sib[a, q, x]
        wait_bytes(xr.at[a, q], rsem.at[a, XRS, q])
        for i in range(3):
            acc = acc + xr[a, q, i].astype(F32)
        osum[a, q] = acc

    def own_out(a):
        def step(i):
            q = (zl + i + 1) % 4
            own_sum(a, q)
            send(osum.at[a, q], orr.at[a, i], a, OOUT, 0, r, 8 * q + xk)

        loop(3, step)
        own_sum(a, zl)

    def total(a):
        wait_bytes(orr.at[a], rsem.at[a, OOUT, 0])
        wait_bytes(zr.at[a], rsem.at[a, ZOUT, 0])
        acc = osum[a, zl]
        for i in range(3):
            acc = acc + orr[a, i]
        for i in range(8):
            acc = acc + zr[a, i].astype(F32)
        return acc.astype(BF)

    def inner(left, right):
        return lax.dot_general(left, right, (((0,), (0,)), ((), ())), preferred_element_type=F32)

    multiply(1, own_id, vec)
    loop(4, lambda q: gather(par_id, pb, 0, q))
    waits = 31 + 15 + 32
    pl.semaphore_wait(
        barrier, waits - 2 * jnp.where(self_z, 1, 0) - 2 * jnp.where(self_out, 1, 0)
    )
    z_in(0, chunk(vec, c))
    loop(4, lambda q: y_out(0, q))
    loop(2, lambda q: z_out(0, q))
    y_in(0, 0, 2)
    z_out(0, 2)
    y_in(0, 2, 2)
    z_out(0, 3)
    y_in(0, 4, 4)
    wait_bytes(up[0].at[pl.ds(0, 3 * QU)], rsem.at[0, YIN, 0])
    multiply(0, par_id, up[0])

    def nth(i):
        return (zl + i + 1) % 4

    def own_gather(a, i):
        gather(own_id, ob, a, nth(i))
        pair_out(a, nth(i))

    def own_products(a):
        own_gather(a, 0)

        def step(i):
            own_gather(a, i + 1)
            x_out(a, nth(i))

        loop(3, step)
        x_out(a, nth(3))

    own_products(0)
    own_out(0)
    first = total(0)
    ach[...] = first

    z_in(1, ach)
    own_in()
    out1[...] = first
    uo[pl.ds(pl.multiple_of(c * CH, CH), CH), :] = first
    gs[pl.ds(0, V), :] = inner(first, first)
    y_in(1, 0, 8)
    wait_bytes(uo.at[pl.ds(0, 28 * CH)], rsem.at[1, OX, 0])
    multiply(1, own_id, uo)

    def partner_step(q):
        gather(par_id, pb, 1, q)

    loop(4, partner_step)
    wait_bytes(up[1].at[pl.ds(0, 3 * QU)], rsem.at[1, YIN, 0])

    gs[pl.ds(V, V), :] = inner(up[1][...], pb[1])

    def gram_out(i):
        to, row, col = level_mate(i)
        send(gs.at[pl.ds(pl.multiple_of(to * 8, 8), 8)], gr1.at[i], 1, G1, 0, row, col)

    loop(31, gram_out)
    loop(4, lambda q: y_out(1, q))
    multiply(0, par_id, up[1])

    own_products(1)
    wait_bytes(gr1, rsem.at[1, G1, 0])
    mine = pl.ds(pl.multiple_of(level * 8, 8), 8)
    gp[...] = lax.fori_loop(0, 31, lambda i, s: s + gr1[i], gs[mine, :])
    loop(15, lambda i: send(gp, gr2.at[i], 1, G2, 0, *line_mate(i)))
    loop(4, lambda q: z_out(1, q))
    own_out(1)
    wait_bytes(gr2, rsem.at[1, G2, 0])
    acc = lax.fori_loop(0, 15, lambda i, s: s + gr2[i], gp[...])
    gf[...] = acc
    loop(31, lambda i: send(gf, ga.at[mine], 1, G3, 0, *level_mate(i)[1:]))
    ga[mine, :] = acc
    out2[...] = total(1)
    wait_bytes(ga.at[pl.ds(0, 2 * V - 8)], rsem.at[1, G3, 0])
    gn[...] = ga[pl.ds(0, V), :] / NROWS
    half = ga[pl.ds(V, V), :]
    gr[...] = (half + half.T) / NROWS

    def sent(a, stage, less, chunks):
        @pl.when(less)
        def _():
            wait_bytes(up[a].at[pl.ds(0, (chunks - 1) * CH)], ssem.at[a, stage])

        @pl.when(jnp.logical_not(less))
        def _():
            wait_bytes(up[a].at[pl.ds(0, chunks * CH)], ssem.at[a, stage])

    for a in range(2):
        sent(a, ZIN, self_z, 8)
        sent(a, ZOUT, self_out, 8)
        wait_bytes(up[a].at[pl.ds(0, 24 * CH)], ssem.at[a, YIN])
        wait_bytes(yr.at[a], ssem.at[a, YRS])
        wait_bytes(sib.at[a], ssem.at[a, SIB])
        wait_bytes(xr.at[a], ssem.at[a, XRS])
        wait_bytes(orr.at[a], ssem.at[a, OOUT])
    wait_bytes(uo.at[pl.ds(0, 3 * CH)], ssem.at[1, OZ])
    wait_bytes(uo.at[pl.ds(0, 28 * CH)], ssem.at[1, OX])
    wait_bytes(gr1, ssem.at[1, G1])
    wait_bytes(gr2, ssem.at[1, G2])
    wait_bytes(gr1, ssem.at[1, G3])


def hand_over(*refs):
    for i in range(4):
        refs[4 + i][...] = refs[i][...]


def body(vectors, tiles, tile_rows, tile_cols):
    vmem = pl.BlockSpec(memory_space=pltpu.VMEM)
    smem = pl.BlockSpec(memory_space=pltpu.SMEM)
    hbm = pl.BlockSpec(memory_space=pltpu.HBM)
    outs = (
        jax.ShapeDtypeStruct((CH, V), BF),
        jax.ShapeDtypeStruct((CH, V), BF),
        jax.ShapeDtypeStruct((V, V), F32),
        jax.ShapeDtypeStruct((V, V), F32),
    )
    results = pl.pallas_call(
        kernel,
        out_shape=outs,
        in_specs=[hbm, hbm, smem, smem],
        out_specs=(vmem,) * 4,
        scratch_shapes=[
            pltpu.VMEM((GROUP, V), BF),
            pltpu.VMEM((K, TS, TS), BF),
            pltpu.VMEM((2, K, TS, TS), BF),
            pltpu.VMEM((GROUP, V), BF),
            pltpu.VMEM((GROUP, V), BF),
            pltpu.VMEM((GROUP, V), BF),
            pltpu.VMEM((K, TS, V), F32),
            pltpu.VMEM((2, GROUP, V), BF),
            pltpu.VMEM((2, GROUP, V), F32),
            pltpu.VMEM((2, 4, 7, CH, V), BF),
            pltpu.VMEM((2, 4, 4, CH, V), F32),
            pltpu.VMEM((2, 4, 3, CH, V), BF),
            pltpu.VMEM((2, 4, 3, CH, V), BF),
            pltpu.VMEM((2, 4, 2, CH, V), BF),
            pltpu.VMEM((2, 8, CH, V), BF),
            pltpu.VMEM((2, 4, CH, V), F32),
            pltpu.VMEM((2, 3, CH, V), F32),
            pltpu.VMEM((CH, V), BF),
            pltpu.VMEM((2 * V, V), F32),
            pltpu.VMEM((NCOL - 1, 8, V), F32),
            pltpu.VMEM((8, V), F32),
            pltpu.VMEM((G - 1, 8, V), F32),
            pltpu.VMEM((8, V), F32),
            pltpu.VMEM((2 * V, V), F32),
            pltpu.SemaphoreType.DMA((2, NSTAGE)),
            pltpu.SemaphoreType.DMA((2, NSTAGE, 8)),
            pltpu.SemaphoreType.DMA((2,)),
        ],
        compiler_params=pltpu.CompilerParams(
            collective_id=0, has_side_effects=True, vmem_limit_bytes=64 * 2**20
        ),
    )(vectors, tiles, tile_rows, tile_cols)
    return pl.pallas_call(
        hand_over,
        out_shape=outs,
        in_specs=[vmem] * 4,
        out_specs=(vmem,) * 4,
        compiler_params=pltpu.CompilerParams(vmem_limit_bytes=64 * 2**20),
    )(*results)


def solution(mesh):
    placed = (P("row", None), P(("row", "col"), None, None), P(("row", "col")), P(("row", "col")))
    return jax.shard_map(
        body,
        mesh=mesh,
        in_specs=placed,
        out_specs=(P(("row", "col"), None), P(("row", "col"), None), P(), P()),
        check_vma=False,
    )
```

```python
import jax
import jax.numpy as jnp
from jax import lax
from jax.experimental import pallas as pl
from jax.experimental.pallas import tpu as pltpu
from jax.sharding import PartitionSpec as P

MESH = pl.DeviceIdType.MESH
BF = jnp.bfloat16
F32 = jnp.float32
TS = 256
V = 128
NB = 12
G = 16
NCOL = 32
K = 8
GROUP = NB * TS
CH = GROUP // NCOL
QU = GROUP // 4
NROWS = GROUP * G

ZIN, YIN, YRS, ZOUT, OZ, OX, OS, SIB, XRS, OOUT, G1, G2, G3 = range(13)
NSTAGE = 13


def loop(n, body):
    def step(i, carry):
        body(i)
        return carry

    lax.fori_loop(0, n, step, 0)


def kernel(
    vec_in, tiles_in, trows, tcols, out1, out2, gn, gr,
    vec, tiles, tt, up0, up1, uo, prod, pb, ob, yr, sib, xs, xr, zs, zr, osum, orr, ach,
    gs, gr1, gp, gr2, gf, ga, ssem, rsem, lsem,
):
    up = (up0, up1)
    r = lax.axis_index("row")
    c = lax.axis_index("col")
    y, zh = r // 4, r % 4
    zl, xk = c // 8, c % 8
    x, k = xk // 2, c % 2
    x1 = x + 1 - 2 * (x % 2)
    par = zl % 2
    p = c % G
    p1 = 8 * par + 2 * x1 + k
    is_high = p <= r
    to_xk = 2 * ((x + 2 * (y // 2)) % 4) + y % 2
    self_z = jnp.logical_and(p == r, y == zl)
    self_out = jnp.logical_and(jnp.logical_or(p == r, p1 == r), to_xk == xk)

    load_vec = pltpu.make_async_copy(vec_in, vec, lsem.at[0])
    load_tiles = pltpu.make_async_copy(tiles_in, tiles, lsem.at[1])
    load_vec.start()
    load_tiles.start()

    def wait_bytes(ref, sem):
        pltpu.make_async_copy(ref, ref, sem).wait()

    def z_group(i):
        j = i // 2
        return 4 * zl + (zh + 2 - j + 3 * (j // 2) - 2 * (j // 3)) % 4, r + G * (i % 2)

    def z_owner(i):
        return p, 8 * y + i

    def out_owner(q, e):
        return (p if e == 0 else p1), 8 * q + to_xk

    rx, rk, rpar = (r // 2) % 4, r % 2, r // 8
    flip = (x % 2 + rx % 2) % 2
    from_y = 2 * ((x // 2 + rx // 2) % 2) + k
    from_x = rx + flip * (1 - 2 * (rx % 2))

    def out_source(i):
        return 4 * from_y + i // 2, 8 * (rpar + 2 * (i % 2)) + 2 * from_x + rk

    def pair_mate(j):
        return 4 * j + zh, 8 * zl + 2 * x1 + k

    level, line = 8 * y + xk, 4 * zh + zl

    def level_mate(i):
        to = (level + i + 1) % 32
        return to, 4 * (to // 8) + zh, 8 * zl + to % 8

    def line_mate(i):
        to = (line + i + 1) % 16
        return 4 * y + to // 4, 8 * (to % 4) + xk

    barrier = pltpu.get_barrier_semaphore()

    def greet(row, col):
        pl.semaphore_signal(barrier, inc=1, device_id=(row, col), device_id_type=MESH)

    def greet_other(row, col):
        @pl.when(jnp.logical_or(row != r, col != c))
        def _():
            greet(row, col)

    loop(8, lambda i: greet_other(*z_group(i)))
    loop(8, lambda i: greet_other(*z_owner(i)))
    loop(4, lambda q: greet_other(*out_owner(q, 0)))
    loop(4, lambda q: greet_other(*out_owner(q, 1)))
    loop(8, lambda i: greet_other(*out_source(i)))
    loop(15, lambda i: greet(*line_mate(i)))
    loop(31, lambda i: greet(*level_mate(i)[1:]))

    straight = jnp.where(is_high, 0, 1)
    load_vec.wait()
    load_tiles.wait()

    def turn(k):
        t = tiles[k]
        tt[straight, k] = t
        tt[1 - straight, k] = t.T

    loop(K, turn)

    def within(block):
        return jnp.minimum(jnp.maximum(block, 0), NB - 1)

    def own_id(k):
        return within(jnp.where(is_high, trows[k], tcols[k]) - r * NB)

    def par_id(k):
        return within(jnp.where(is_high, tcols[k], trows[k]) - p * NB)

    def send(src, dst, a, stage, sub, row, col):
        pltpu.make_async_remote_copy(
            src_ref=src,
            dst_ref=dst,
            send_sem=ssem.at[a, stage],
            recv_sem=rsem.at[a, stage, sub],
            device_id=(row, col),
            device_id_type=MESH,
        ).start()

    def send_or_copy(src, dst, a, stage, sub, row, col):
        same = jnp.logical_and(row == r, col == c)

        @pl.when(same)
        def _():
            pltpu.make_async_copy(src, dst, rsem.at[a, stage, sub]).start()

        @pl.when(jnp.logical_not(same))
        def _():
            send(src, dst, a, stage, sub, row, col)

    def chunk(ref, i):
        return ref.at[pl.ds(pl.multiple_of(i * CH, CH), CH)]

    def read(ref, a, i):
        return ref[a, pl.ds(pl.multiple_of(i * CH, CH), CH), :].astype(F32)

    def z_in(a, src):
        loop(8, lambda i: send_or_copy(src, chunk(up[a], c), a, ZIN, xk, *z_group(i)))

    def y_in(a, first, count):
        def forward(i):
            part = chunk(up[a], 8 * y + first + i)
            wait_bytes(part, rsem.at[a, ZIN, first + i])
            loop(3, lambda j: send(part, part, a, YIN, 0, 4 * ((y + j + 1) % 4) + zh, c))

        loop(count, forward)

    def to_sibling(src, where):
        send(src, chunk(uo, where), 1, OS, 0, r, c + 1 - 2 * k)

    def spread(src, where, group):
        loop(3, lambda i: send(src, chunk(uo, where), 1, OX, group, r, 8 * zl + 2 * ((x + i + 1) % 4) + k))
        to_sibling(src, where)

    def own_in():
        loop(3, lambda i: send(ach, chunk(uo, c), 1, OZ, i, r, 8 * ((zl + i + 1) % 4) + xk))
        spread(ach, c, 0)

        def forward(i):
            cc = 8 * ((zl + 3 - i) % 4) + xk
            part = chunk(uo, cc)
            wait_bytes(part, rsem.at[1, OZ, i])
            spread(part, cc, 1 + i)

        loop(3, forward)

        def across(g):
            wait_bytes(uo.at[pl.ds(0, 3 * CH)], rsem.at[1, OX, g])

            def one(i):
                cc = 8 * ((zl + 4 - g) % 4) + 2 * ((x + i + 1) % 4) + k
                to_sibling(chunk(uo, cc), cc)

            loop(3, one)

        return across

    def one_if_same(left, right):
        gap = left - right
        return (1 - jnp.minimum(gap * gap, 1)).astype(F32)

    def multiply(side, ids_from, source):
        def one(k):
            block = source[pl.ds(ids_from(k) * TS, TS), :]
            prod[k] = jnp.dot(tt[side, k], block, preferred_element_type=F32)

        loop(K, one)

    def gather(ids_to, target, a, q):
        def block(i):
            b = 3 * q + i
            weights = [one_if_same(ids_to(k), b) for k in range(K)]
            for s in range(4):
                piece = pl.ds(64 * s, 64)
                acc = prod[0, piece, :] * weights[0]
                for k in range(1, K):
                    acc = acc + prod[k, piece, :] * weights[k]
                target[a, pl.ds(pl.multiple_of(b * TS + 64 * s, 64), 64), :] = acc.astype(target.dtype)

        loop(3, block)

    def y_out(a, q):
        def mate(i):
            j = (y + i + 1) % 4
            part = chunk(pb.at[a], 8 * q + 2 * ((x + 2 * (j // 2)) % 4) + j % 2)
            send(part, yr.at[a, q, i], a, YRS, q, 4 * j + zh, c)

        def pair(i):
            j = (y + i) % 4
            part = chunk(pb.at[a], 8 * q + 2 * ((x1 + 2 * (j // 2)) % 4) + j % 2)
            send(part, yr.at[a, q, 3 + i], a, YRS, q, *pair_mate(j))

        loop(4, pair)
        loop(3, mate)

    def z_out(a, q):
        slot = zh * 2 + c // G
        wait_bytes(yr.at[a, q], rsem.at[a, YRS, q])
        acc = read(pb, a, 8 * q + to_xk)
        for i in range(3):
            acc = acc + yr[a, q, i].astype(F32)
        zs[a, q, 0] = acc.astype(BF)
        acc = yr[a, q, 3].astype(F32)
        for i in range(4, 7):
            acc = acc + yr[a, q, i].astype(F32)
        zs[a, q, 1] = acc.astype(BF)
        send_or_copy(zs.at[a, q, 0], zr.at[a, slot], a, ZOUT, 0, *out_owner(q, 0))
        send_or_copy(zs.at[a, q, 1], zr.at[a, slot], a, ZOUT, 0, *out_owner(q, 1))

    def pair_out(a, q):
        def piece(i):
            part = chunk(ob.at[a], 8 * q + 2 * i + 1 - k)
            send(part, sib.at[a, q, i], a, SIB, q, r, 8 * zl + 2 * x + 1 - k)

        loop(4, piece)

    def x_out(a, q):
        wait_bytes(sib.at[a, q], rsem.at[a, SIB, q])

        def mate(i):
            to = (x + i + 1) % 4
            xs[a, q, i] = (read(ob, a, 8 * q + 2 * to + k) + sib[a, q, to]).astype(BF)
            send(xs.at[a, q, i], xr.at[a, q, i], a, XRS, q, r, 8 * zl + 2 * to + k)

        loop(3, mate)

    def own_sum(a, q):
        acc = read(ob, a, 8 * q + xk) + sib[a, q, x]
        wait_bytes(xr.at[a, q], rsem.at[a, XRS, q])
        for i in range(3):
            acc = acc + xr[a, q, i].astype(F32)
        osum[a, q] = acc

    def own_out(a):
        def step(i):
            q = (zl + i + 1) % 4
            own_sum(a, q)
            send(osum.at[a, q], orr.at[a, i], a, OOUT, 0, r, 8 * q + xk)

        loop(3, step)
        own_sum(a, zl)

    def total(a):
        wait_bytes(orr.at[a], rsem.at[a, OOUT, 0])
        wait_bytes(zr.at[a], rsem.at[a, ZOUT, 0])
        acc = osum[a, zl]
        for i in range(3):
            acc = acc + orr[a, i]
        for i in range(8):
            acc = acc + zr[a, i].astype(F32)
        return acc.astype(BF)

    def inner(left, right):
        return lax.dot_general(left, right, (((0,), (0,)), ((), ())), preferred_element_type=F32)

    multiply(1, own_id, vec)
    loop(4, lambda q: gather(par_id, pb, 0, q))
    waits = 31 + 15 + 32
    pl.semaphore_wait(
        barrier, waits - 2 * jnp.where(self_z, 1, 0) - 2 * jnp.where(self_out, 1, 0)
    )
    z_in(0, chunk(vec, c))
    loop(4, lambda q: y_out(0, q))
    loop(2, lambda q: z_out(0, q))
    y_in(0, 0, 2)
    z_out(0, 2)
    y_in(0, 2, 2)
    z_out(0, 3)
    y_in(0, 4, 4)
    wait_bytes(up[0].at[pl.ds(0, 3 * QU)], rsem.at[0, YIN, 0])
    multiply(0, par_id, up[0])

    def nth(i):
        return (zl + i + 1) % 4

    def own_gather(a, i):
        gather(own_id, ob, a, nth(i))
        pair_out(a, nth(i))

    def own_products(a):
        own_gather(a, 0)

        def step(i):
            own_gather(a, i + 1)
            x_out(a, nth(i))

        loop(3, step)
        x_out(a, nth(3))

    own_products(0)
    own_out(0)
    first = total(0)
    ach[...] = first

    z_in(1, ach)
    across = own_in()
    out1[...] = first
    uo[pl.ds(pl.multiple_of(c * CH, CH), CH), :] = first
    gs[pl.ds(0, V), :] = inner(first, first)
    y_in(1, 0, 8)
    loop(4, across)
    wait_bytes(uo.at[pl.ds(0, 16 * CH)], rsem.at[1, OS, 0])
    multiply(1, own_id, uo)

    def partner_step(q):
        gather(par_id, pb, 1, q)

    loop(4, partner_step)
    wait_bytes(up[1].at[pl.ds(0, 3 * QU)], rsem.at[1, YIN, 0])

    gs[pl.ds(V, V), :] = inner(up[1][...], pb[1])

    def gram_out(i):
        to, row, col = level_mate(i)
        send(gs.at[pl.ds(pl.multiple_of(to * 8, 8), 8)], gr1.at[i], 1, G1, 0, row, col)

    loop(31, gram_out)
    loop(4, lambda q: y_out(1, q))
    multiply(0, par_id, up[1])

    own_products(1)
    wait_bytes(gr1, rsem.at[1, G1, 0])
    mine = pl.ds(pl.multiple_of(level * 8, 8), 8)
    gp[...] = lax.fori_loop(0, 31, lambda i, s: s + gr1[i], gs[mine, :])
    loop(15, lambda i: send(gp, gr2.at[i], 1, G2, 0, *line_mate(i)))
    loop(4, lambda q: z_out(1, q))
    own_out(1)
    wait_bytes(gr2, rsem.at[1, G2, 0])
    acc = lax.fori_loop(0, 15, lambda i, s: s + gr2[i], gp[...])
    gf[...] = acc
    loop(31, lambda i: send(gf, ga.at[mine], 1, G3, 0, *level_mate(i)[1:]))
    ga[mine, :] = acc
    out2[...] = total(1)
    wait_bytes(ga.at[pl.ds(0, 2 * V - 8)], rsem.at[1, G3, 0])
    gn[...] = ga[pl.ds(0, V), :] / NROWS
    half = ga[pl.ds(V, V), :]
    gr[...] = (half + half.T) / NROWS

    def sent(a, stage, less, chunks):
        @pl.when(less)
        def _():
            wait_bytes(up[a].at[pl.ds(0, (chunks - 1) * CH)], ssem.at[a, stage])

        @pl.when(jnp.logical_not(less))
        def _():
            wait_bytes(up[a].at[pl.ds(0, chunks * CH)], ssem.at[a, stage])

    for a in range(2):
        sent(a, ZIN, self_z, 8)
        sent(a, ZOUT, self_out, 8)
        wait_bytes(up[a].at[pl.ds(0, 24 * CH)], ssem.at[a, YIN])
        wait_bytes(yr.at[a], ssem.at[a, YRS])
        wait_bytes(sib.at[a], ssem.at[a, SIB])
        wait_bytes(xr.at[a], ssem.at[a, XRS])
        wait_bytes(orr.at[a], ssem.at[a, OOUT])
    wait_bytes(uo.at[pl.ds(0, 3 * CH)], ssem.at[1, OZ])
    wait_bytes(uo.at[pl.ds(0, 12 * CH)], ssem.at[1, OX])
    wait_bytes(uo.at[pl.ds(0, 16 * CH)], ssem.at[1, OS])
    wait_bytes(gr1, ssem.at[1, G1])
    wait_bytes(gr2, ssem.at[1, G2])
    wait_bytes(gr1, ssem.at[1, G3])


def hand_over(*refs):
    for i in range(4):
        refs[4 + i][...] = refs[i][...]


def body(vectors, tiles, tile_rows, tile_cols):
    vmem = pl.BlockSpec(memory_space=pltpu.VMEM)
    smem = pl.BlockSpec(memory_space=pltpu.SMEM)
    hbm = pl.BlockSpec(memory_space=pltpu.HBM)
    outs = (
        jax.ShapeDtypeStruct((CH, V), BF),
        jax.ShapeDtypeStruct((CH, V), BF),
        jax.ShapeDtypeStruct((V, V), F32),
        jax.ShapeDtypeStruct((V, V), F32),
    )
    results = pl.pallas_call(
        kernel,
        out_shape=outs,
        in_specs=[hbm, hbm, smem, smem],
        out_specs=(vmem,) * 4,
        scratch_shapes=[
            pltpu.VMEM((GROUP, V), BF),
            pltpu.VMEM((K, TS, TS), BF),
            pltpu.VMEM((2, K, TS, TS), BF),
            pltpu.VMEM((GROUP, V), BF),
            pltpu.VMEM((GROUP, V), BF),
            pltpu.VMEM((GROUP, V), BF),
            pltpu.VMEM((K, TS, V), F32),
            pltpu.VMEM((2, GROUP, V), BF),
            pltpu.VMEM((2, GROUP, V), F32),
            pltpu.VMEM((2, 4, 7, CH, V), BF),
            pltpu.VMEM((2, 4, 4, CH, V), F32),
            pltpu.VMEM((2, 4, 3, CH, V), BF),
            pltpu.VMEM((2, 4, 3, CH, V), BF),
            pltpu.VMEM((2, 4, 2, CH, V), BF),
            pltpu.VMEM((2, 8, CH, V), BF),
            pltpu.VMEM((2, 4, CH, V), F32),
            pltpu.VMEM((2, 3, CH, V), F32),
            pltpu.VMEM((CH, V), BF),
            pltpu.VMEM((2 * V, V), F32),
            pltpu.VMEM((NCOL - 1, 8, V), F32),
            pltpu.VMEM((8, V), F32),
            pltpu.VMEM((G - 1, 8, V), F32),
            pltpu.VMEM((8, V), F32),
            pltpu.VMEM((2 * V, V), F32),
            pltpu.SemaphoreType.DMA((2, NSTAGE)),
            pltpu.SemaphoreType.DMA((2, NSTAGE, 8)),
            pltpu.SemaphoreType.DMA((2,)),
        ],
        compiler_params=pltpu.CompilerParams(
            collective_id=0, has_side_effects=True, vmem_limit_bytes=64 * 2**20
        ),
    )(vectors, tiles, tile_rows, tile_cols)
    return pl.pallas_call(
        hand_over,
        out_shape=outs,
        in_specs=[vmem] * 4,
        out_specs=(vmem,) * 4,
        compiler_params=pltpu.CompilerParams(vmem_limit_bytes=64 * 2**20),
    )(*results)


def solution(mesh):
    placed = (P("row", None), P(("row", "col"), None, None), P(("row", "col")), P(("row", "col")))
    return jax.shard_map(
        body,
        mesh=mesh,
        in_specs=placed,
        out_specs=(P(("row", "col"), None), P(("row", "col"), None), P(), P()),
        check_vma=False,
    )
```
